256 devices in a mesh: sample: 32 (over x_lo, z, core), block: 8 (over x_hi, y).
Axes of the slice: x: 4 (x_hi: 2, x_lo: 2; x = x_hi * 2 + x_lo), y: 4, z: 8, core: 2. Of those that a mesh axis runs over, the one named last changes fastest.
Arguments:
- genotype: int32 [32768, 8000], P('sample', 'block'), may hold values from 0 to 2
- allele_freq: float32 [8000], P('block'), may hold values from 0.05 to 0.5
- phenotype: bfloat16 [32768, 16], P('sample'), may hold values from -6 to 6
- shrinkage: float32 [2], replicated, may hold values from 0.05 to 2
- owner_order: int32 [16], replicated, may hold values from 0 to 15, each once
Outputs:
- predictions: bfloat16 [16, 32, 32768], P('block', None, 'sample')
The draws below stay inside these ranges and needn't reach their ends.
Inputs may be any that keep to these rules, and one draw needn't show every extreme that they name: `owner_order`: each phenotype appears once.
All inputs are finite; a program needn't handle non-finite values.
Results may differ from the reference program's by a relative error of at most 0.0056.
Values may be sent and summed in bfloat16 or wider, within the bound.
A program may use at most 128 MiB of HBM per device.

```python
import jax
import jax.numpy as jnp
from jax import lax

SNPS = 500
PHENOS = 16
RIDGES = 2
FOLDS = 5
TOTAL_SAMPLES = 32768
BLOCKS = 16
SNP_TOTAL = 8000


def cohort(key):
    percent = jax.random.randint(jax.random.fold_in(key, 11), (SNP_TOTAL,), 5, 51)
    percent = percent.at[0].set(5).at[1].set(50)
    weight_key = jax.random.fold_in(key, 13)

    def one_block(column):
        block_key = jax.random.fold_in(jax.random.fold_in(key, 17), column)
        offset = (column * SNPS).astype(jnp.int32)
        cutoff = lax.dynamic_slice_in_dim(percent, offset, SNPS)
        positions = lax.broadcasted_iota(jnp.int32, (TOTAL_SAMPLES, SNPS), 1)
        dosage = jnp.zeros((TOTAL_SAMPLES, SNPS), jnp.int32)
        for strand in range(2):
            strand_key = jax.random.fold_in(block_key, strand)
            renewed = jax.random.randint(jax.random.fold_in(strand_key, 1), (TOTAL_SAMPLES, SNPS), 0, 64) == 0
            renewed = jnp.logical_or(renewed, positions == 0)
            anchor = lax.cummax(jnp.where(renewed, positions, 0), axis=1)
            ticket = jax.random.randint(jax.random.fold_in(strand_key, 2), (TOTAL_SAMPLES, SNPS), 0, 100)
            carried = jnp.take_along_axis(ticket, anchor, axis=1)
            dosage = dosage + (carried < cutoff[None, :]).astype(jnp.int32)
        frequency = cutoff.astype(jnp.float32) / 100.0
        scaled = (dosage.astype(jnp.float32) - 2.0 * frequency) / jnp.sqrt(2.0 * frequency * (1.0 - frequency))
        effect = jax.random.normal(jax.random.fold_in(weight_key, column), (SNPS, PHENOS), jnp.float32)
        return (dosage, jnp.dot(scaled, effect, precision=lax.Precision.HIGHEST))
    dosages, shares = lax.map(one_block, jnp.arange(BLOCKS, dtype=jnp.int32))
    genetic = jnp.sum(shares, axis=0)
    genotype = jnp.transpose(dosages, (1, 0, 2)).reshape(TOTAL_SAMPLES, SNP_TOTAL)
    return (genotype, percent, genetic)


def draw_genotype(key, part):
    return cohort(key)[0]


def draw_allele_freq(key, part):
    return cohort(key)[1].astype(jnp.float32) / 100.0


def draw_phenotype(key, part):
    genetic = cohort(key)[2]
    centered = genetic - jnp.mean(genetic, axis=0)
    spread = jnp.sqrt(jnp.mean(centered * centered, axis=0))
    signal = centered / spread
    residue_key = jax.random.fold_in(key, 19)
    herit_key = jax.random.fold_in(key, 23)
    heritable = jax.random.uniform(herit_key, (PHENOS,), jnp.float32, 0.3, 0.8)
    residue = jax.random.normal(residue_key, (TOTAL_SAMPLES, PHENOS), jnp.float32)
    traits = jnp.sqrt(heritable) * signal + jnp.sqrt(1.0 - heritable) * residue
    return jnp.clip(traits, -6.0, 6.0).astype(jnp.bfloat16)


def draw_shrinkage(key, part):
    fraction = jax.random.uniform(jax.random.fold_in(key, 31), (2,), jnp.float32, 0.0, 1.0)
    small_lo, small_hi, large_lo, large_hi = (0.05, 0.08, 0.5, 2.0)
    small_value = small_lo * jnp.exp(fraction[0] * jnp.log(small_hi / small_lo))
    large_value = large_lo * jnp.exp(fraction[1] * jnp.log(large_hi / large_lo))
    flip = jax.random.randint(jax.random.fold_in(key, 37), (), 0, 2)
    first = jnp.where(flip == 1, large_value, small_value)
    second = jnp.where(flip == 1, small_value, large_value)
    return jnp.clip(jnp.stack([first, second]), 0.05, 2.0).astype(jnp.float32)


def setup_inputs(seed: int = 0) -> dict:
    key_list = jax.random.split(jax.random.key(seed), 6)
    return {
        "genotype": draw_genotype(jax.random.fold_in(key_list[5], 71), 0),
        "allele_freq": draw_allele_freq(jax.random.fold_in(key_list[5], 71), 0),
        "phenotype": draw_phenotype(jax.random.fold_in(key_list[5], 71), 0),
        "shrinkage": draw_shrinkage(jax.random.fold_in(key_list[5], 71), 0),
        "owner_order": jax.random.permutation(key_list[4], PHENOS).astype(jnp.int32),
    }


def standardize(genotype, allele_freq):
    spread = jnp.sqrt(2.0 * allele_freq * (1.0 - allele_freq))
    return ((genotype.astype(jnp.float32) - 2.0 * allele_freq) / spread).astype(jnp.bfloat16)

def solve_pair(factor, target):
    return jax.scipy.linalg.cho_solve((factor, True), target)

def ridge_solve(grams, crosses, shrinkage, counts):
    lead = grams.shape[:2]
    width = grams.shape[-1]
    system = grams / counts[:, None, None, None]
    target = crosses / counts[:, None, None, None]
    system = system.reshape(-1, width, width)
    target = target.reshape(-1, width, crosses.shape[-1])
    identity = jnp.eye(width, dtype=jnp.float32)
    full = system[:, None] + shrinkage[None, :, None, None] * identity
    factor = jnp.linalg.cholesky(full)
    per_ridge = jax.vmap(solve_pair, (0, None))
    solved = jax.vmap(per_ridge, (0, 0))(factor, target)
    return solved.reshape(lead + solved.shape[1:])

def predict(columns, weights):
    stacked = jnp.transpose(weights, (2, 0, 1)).reshape(-1, weights.shape[1])
    product = lax.dot_general(stacked.astype(jnp.float32), columns.astype(jnp.float32), (((1,), (1,)), ((), ())), preferred_element_type=jnp.float32)
    return product.astype(jnp.bfloat16).reshape(weights.shape[2], weights.shape[0], columns.shape[0])

def fold_bounds(total):
    return [-(-(k * total) // FOLDS) for k in range(FOLDS + 1)]

def reference(genotype, allele_freq, phenotype, shrinkage, owner_order):
    scaled = standardize(genotype, allele_freq)
    ordered = jnp.take(phenotype, owner_order, axis=1)
    bounds = fold_bounds(TOTAL_SAMPLES)
    sizes_list = [float(TOTAL_SAMPLES - (bounds[k + 1] - bounds[k])) for k in range(FOLDS)]
    counts = jnp.array(sizes_list, dtype=jnp.float32)

    def block_sums(column):
        offset = (column * SNPS).astype(jnp.int32)
        columns = lax.dynamic_slice_in_dim(scaled, offset, SNPS, 1)
        gram_list = []
        cross_list = []
        for k in range(FOLDS):
            part_cols = columns[bounds[k]:bounds[k + 1]]
            part_traits = ordered[bounds[k]:bounds[k + 1]]
            gram_list.append(lax.dot_general(part_cols.astype(jnp.float32), part_cols.astype(jnp.float32), (((0,), (0,)), ((), ())), preferred_element_type=jnp.float32))
            cross_list.append(lax.dot_general(part_cols.astype(jnp.float32), part_traits.astype(jnp.float32), (((0,), (0,)), ((), ())), preferred_element_type=jnp.float32))
        return (jnp.stack(gram_list), jnp.stack(cross_list))
    grams, crosses = lax.map(block_sums, jnp.arange(BLOCKS, dtype=jnp.int32))
    grams = jnp.transpose(grams, (1, 0, 2, 3))
    crosses = jnp.transpose(crosses, (1, 0, 2, 3))
    rest_grams = lax.optimization_barrier(jnp.sum(grams, axis=0))[None] - grams
    rest_crosses = lax.optimization_barrier(jnp.sum(crosses, axis=0))[None] - crosses
    weights = ridge_solve(rest_grams, rest_crosses, shrinkage, counts).astype(jnp.bfloat16)
    weights = jnp.transpose(weights, (1, 0, 2, 3, 4))

    def block_predictions(packed):
        column, block_weights = packed
        offset = (column * SNPS).astype(jnp.int32)
        columns = lax.dynamic_slice_in_dim(scaled, offset, SNPS, 1)
        pieces = [predict(columns[bounds[k]:bounds[k + 1]], block_weights[k]) for k in range(FOLDS)]
        return jnp.concatenate(pieces, axis=2)
    predictions = lax.map(block_predictions, (jnp.arange(BLOCKS, dtype=jnp.int32), weights))
    return jnp.transpose(predictions, (1, 0, 2, 3)).reshape(PHENOS, BLOCKS * RIDGES, TOTAL_SAMPLES)
```

```python
import functools

import jax
import jax.numpy as jnp
from jax import lax
from jax.experimental import pallas as pl
from jax.experimental.pallas import tpu as pltpu
from jax.sharding import PartitionSpec as P

SNPS = 500
FOLDS = 5
WIDE = 512
ROWS = 1024
CHIPS = 16
SLICE = 80
OUT_LANES = 512
MESH = pl.DeviceIdType.MESH
BF16 = jnp.bfloat16
I16 = jnp.int16

W = 128
TRAITS = 16
PAIRS = [(i, j) for i in range(4) for j in range(i, 4)]
F32 = jnp.float32
HI = lax.Precision.HIGHEST


def row_of(x, i):
    return jnp.broadcast_to(x[i : i + 1, :], x.shape)


def lane_of(x, k):
    return jnp.broadcast_to(x[:, k : k + 1], x.shape)


def invert(tiles):
    sub = lax.broadcasted_iota(jnp.int32, (8, W), 0)
    lane = lax.broadcasted_iota(jnp.int32, (8, W), 1)
    for j in range(16):
        inside = (lane >= 8 * j) & (lane < 8 * j + 8)
        panel = tiles[j]
        cols = [lane_of(panel, 8 * j + i) for i in range(8)]
        rows = jnp.where(inside, (lane - 8 * j == sub).astype(F32), panel)
        for i in range(8):
            here = sub == i
            recip = 1.0 / row_of(cols[i], i)
            q = row_of(rows, i) * recip
            rows = jnp.where(here, q, rows - cols[i] * q)
            for c in range(i + 1, 8):
                qc = row_of(cols[c], i) * recip
                cols[c] = jnp.where(here, qc, cols[c] - cols[i] * qc)
        spread = [row_of(rows, i) for i in range(8)]
        new = []
        for t in range(16):
            if t == j:
                new.append(rows)
                continue
            acc = lane_of(tiles[t], 8 * j) * spread[0]
            for i in range(1, 8):
                acc = acc + lane_of(tiles[t], 8 * j + i) * spread[i]
            new.append(jnp.where(inside, 0.0, tiles[t]) - acc)
        tiles = new
    return tiles


def solve_kernel(par_ref, gram_ref, cross_ref, vec_ref, out_ref, m_ref, c_ref, t_ref, d_ref):
    lam = par_ref[0]
    inv_n = 1.0 / par_ref[1]
    count = par_ref[1]
    eye = lax.broadcasted_iota(jnp.int32, (W, W), 0) == lax.broadcasted_iota(jnp.int32, (W, W), 1)
    a_row = [vec_ref[2:3, W * t : W * t + W] for t in range(4)]
    w_row = [vec_ref[3:4, W * t : W * t + W] for t in range(4)]

    def turn(row):
        return jnp.sum(jnp.where(eye, jnp.broadcast_to(row, (W, W)), 0.0), axis=1, keepdims=True)

    a_col = [turn(r) for r in a_row]
    w_col = [turn(r) for r in w_row]
    u_col = []
    v_row = []
    for t in range(4):
        at = PAIRS.index((t, 3)) * W
        u = gram_ref[at : at + W, :].astype(F32)[:, 116:117]
        u_col.append(u)
        u_row = jnp.sum(jnp.where(eye, jnp.broadcast_to(u, (W, W)), 0.0), axis=0, keepdims=True)
        v_row.append(u_row - count * a_row[t])
    for at, (i, j) in enumerate(PAIRS):
        s = gram_ref[W * at : W * at + W, :].astype(F32)
        x = (s - u_col[i] * a_row[j] - a_col[i] * v_row[j]) * (w_col[i] * inv_n) * w_row[j]
        if i == j:
            if i == 3:
                pad = (lax.broadcasted_iota(jnp.int32, (W, W), 0) >= 116).astype(F32)
                x = x + jnp.where(eye, pad + lam, 0.0)
            else:
                x = x + jnp.where(eye, lam, 0.0)
        m_ref[i, :, W * j : W * j + W] = x
    total = cross_ref[96 : 96 + TRAITS, 116:117]
    for t in range(4):
        c = cross_ref[32 * t : 32 * t + TRAITS, :]
        c_ref[:, W * t : W * t + W] = (c - total * a_row[t]) * (w_row[t] * inv_n)

    dot = functools.partial(lax.dot_general, precision=HI, preferred_element_type=F32)
    nn = (((1,), (0,)), ((), ()))
    tn = (((0,), (0,)), ((), ()))
    nt = (((1,), (1,)), ((), ()))
    d_ref[...] = m_ref[0, :, 0:W]

    def step(b, carry):
        tiles = invert([d_ref[8 * t : 8 * t + 8, :] for t in range(16)])
        for t in range(16):
            d_ref[8 * t : 8 * t + 8, :] = tiles[t]
        for s in range(4):
            @pl.when(b == s)
            def _():
                dinv = d_ref[...]
                lo = W * (s + 1)
                y = dot(c_ref[:, lo - W : lo], dinv, nn)
                c_ref[:, lo - W : lo] = y
                if s < 3:
                    right = m_ref[s, :, lo:]
                    t_new = dot(dinv, right, nn)
                    t_ref[s, :, lo:] = t_new
                    c_ref[:, lo:] = c_ref[:, lo:] - dot(y, right, nn)
                    for i in range(s + 1, 4):
                        left = m_ref[s, :, W * i : W * i + W]
                        m_ref[i, :, W * i :] = m_ref[i, :, W * i :] - dot(left, t_ref[s, :, W * i :], tn)
                    d_ref[...] = m_ref[s + 1, :, lo : lo + W]
        return carry

    lax.fori_loop(0, 4, step, 0)
    for s in (2, 1, 0):
        lo = W * (s + 1)
        c_ref[:, lo - W : lo] = c_ref[:, lo - W : lo] - dot(c_ref[:, lo:], t_ref[s, :, lo:], nt)
    out_ref[...] = c_ref[...].astype(jnp.bfloat16)


def solve(par, gram, cross, vec):
    return pl.pallas_call(
        solve_kernel,
        out_shape=jax.ShapeDtypeStruct((TRAITS, 512), jnp.bfloat16),
        in_specs=[pl.BlockSpec(memory_space=pltpu.SMEM)] + [pl.BlockSpec(memory_space=pltpu.VMEM)] * 3,
        out_specs=pl.BlockSpec(memory_space=pltpu.VMEM),
        scratch_shapes=[
            pltpu.VMEM((4, W, 512), F32),
            pltpu.VMEM((TRAITS, 512), F32),
            pltpu.VMEM((4, W, 512), F32),
            pltpu.VMEM((W, W), F32),
        ],
        compiler_params=pltpu.CompilerParams(vmem_limit_bytes=32 * 1024 * 1024),
    )(par, gram, cross, vec)


VMEM = pl.BlockSpec(memory_space=pltpu.VMEM)
SMEM = pl.BlockSpec(memory_space=pltpu.SMEM)
LIMIT = 48 * 1024 * 1024


def bounds():
    return [-(-(k * ROWS * 2 * CHIPS) // FOLDS) for k in range(FOLDS + 1)]


def first_fold(chip):
    return [k for k in range(FOLDS) if bounds()[k] <= chip * 2 * ROWS < bounds()[k + 1]][0]


STRADDLE = [c for c in range(CHIPS) if bounds()[first_fold(c) + 1] < (c + 1) * 2 * ROWS]


def gram_kernel(par_ref, order_ref, geno_ref, pheno_ref, vec_ref, part_ref, cross_ref, x_ref, g_ref, y_ref):
    bound = par_ref[0]
    lane = lax.broadcasted_iota(jnp.int32, (128, WIDE), 1)

    def chunk(i, carry):
        at = pl.multiple_of(i * 128, 128)
        for b in range(2):
            raw = geno_ref[pl.ds(at, 128), b * SNPS : (b + 1) * SNPS].astype(F32)
            raw = jnp.concatenate([raw, jnp.ones((128, WIDE - SNPS), F32)], axis=1)
            two_p = vec_ref[0:1, b * WIDE : (b + 1) * WIDE]
            spread = vec_ref[1:2, b * WIDE : (b + 1) * WIDE]
            x_ref[pl.ds(at, 128), b * WIDE : (b + 1) * WIDE] = ((raw - two_p) / spread).astype(BF16)
            g_ref[b, pl.ds(at, 128), :] = jnp.where(lane == SNPS, 1.0, raw - 1.0).astype(BF16)
        return carry

    lax.fori_loop(0, ROWS // 128, chunk, 0)
    rows = lax.broadcasted_iota(jnp.int32, (16, 32), 0)
    cols = lax.broadcasted_iota(jnp.int32, (16, 32), 1)
    pick = jnp.zeros((16, 32), F32)
    for q in range(TRAITS):
        pick = jnp.where((cols == q) & (rows == order_ref[q]), 1.0, pick)
    y_ref[...] = jnp.dot(pheno_ref[...], pick.astype(BF16), preferred_element_type=F32).astype(BF16)
    tn = (((0,), (0,)), ((), ()))
    row_ids = lax.broadcasted_iota(jnp.int32, (ROWS, 128), 0)
    for slot in range(2):
        def fill(slot=slot):
            keep = (row_ids < bound) if slot == 0 else (row_ids >= bound)
            y = jnp.where(keep[:, :32], y_ref[...], jnp.zeros((ROWS, 32), BF16))
            for b in range(2):
                at = 0
                for i in range(4):
                    left = g_ref[b, :, 128 * i : 128 * i + 128]
                    left = jnp.where(keep, left, jnp.zeros_like(left))
                    out = lax.dot_general(left, g_ref[b, :, 128 * i :], tn, preferred_element_type=F32)
                    out = out.astype(jnp.int32).astype(I16)
                    for j in range(4 - i):
                        part_ref[b, slot, at : at + 128, :] = out[:, 128 * j : 128 * j + 128]
                        at += 128
                out = lax.dot_general(y, g_ref[b], tn, preferred_element_type=F32)
                for t in range(4):
                    cross_ref[b, slot, 32 * t : 32 * t + 32, :] = out[:, 128 * t : 128 * t + 128]
        if slot == 0:
            fill()
        else:
            pl.when(bound < 2 * ROWS)(fill)


def grams(par, order, geno, pheno, vec):
    return pl.pallas_call(
        gram_kernel,
        out_shape=[
            jax.ShapeDtypeStruct((2, 2, CHIPS * SLICE, 128), I16),
            jax.ShapeDtypeStruct((2, 2, 128, 128), F32),
            jax.ShapeDtypeStruct((ROWS, 2 * WIDE), BF16),
        ],
        in_specs=[SMEM, SMEM, VMEM, VMEM, VMEM],
        out_specs=[VMEM, VMEM, VMEM],
        scratch_shapes=[pltpu.VMEM((2, ROWS, WIDE), BF16), pltpu.VMEM((ROWS, 32), BF16)],
        compiler_params=pltpu.CompilerParams(vmem_limit_bytes=LIMIT),
    )(par, order, geno, pheno, vec)


def remote(src, dst, send, recv, sample):
    return pltpu.make_async_remote_copy(
        src_ref=src, dst_ref=dst, send_sem=send, recv_sem=recv, device_id={"sample": sample}, device_id_type=MESH
    )


def reduce_kernel(
    part_ref, cross_ref, gram_ref, rhs_ref,
    sib, sib_x, mine, mine_x, got, got_x, got_b, got_xb, rest, rest_x,
    sib_sem, a_send, a_recv, b_send, b_recv, r_send, r_recv,
):
    me = lax.axis_index("sample")
    core = lax.rem(me, 2)
    chip = me // 2
    other = me + 1 - 2 * core
    straddles = (lax.rem(chip, 3) == 0) & (chip > 0) & (chip < 15)
    solver = (lax.rem(chip, 3) < 2) & (chip < 15)
    barrier = pltpu.get_barrier_semaphore()
    pl.semaphore_signal(barrier, inc=1, device_id={"sample": other}, device_id_type=MESH)
    for d in range(1, CHIPS):
        peer = 2 * lax.rem(chip + d, CHIPS) + core
        pl.semaphore_signal(barrier, inc=1, device_id={"sample": peer}, device_id_type=MESH)
    pl.semaphore_wait(barrier, CHIPS)

    def sibling(slot):
        return (
            remote(part_ref.at[1 - core, slot], sib.at[slot], sib_sem.at[0, slot], sib_sem.at[1, slot], other),
            remote(cross_ref.at[1 - core, slot], sib_x.at[slot], sib_sem.at[2, slot], sib_sem.at[3, slot], other),
        )

    def start_sibling(slot):
        for c in sibling(slot):
            c.start()

    def merge(slot):
        for c in sibling(slot):
            c.wait()

        def add(o, carry):
            at = pl.multiple_of(o * SLICE, 16)
            left = part_ref[core, slot, pl.ds(at, SLICE), :].astype(jnp.int32)
            right = sib[slot, pl.ds(at, SLICE), :].astype(jnp.int32)
            mine[slot, o] = (left + right).astype(I16)
            return carry

        lax.fori_loop(0, CHIPS, add, 0)
        for o in range(CHIPS):
            mine_x[slot, o] = cross_ref[core, slot, 8 * o : 8 * o + 8, :] + sib_x[slot, 8 * o : 8 * o + 8, :]

    def send_a(o, source):
        return (
            remote(mine.at[0, o], got.at[source], a_send.at[0, o], a_recv.at[0, source], 2 * o + core),
            remote(mine_x.at[0, o], got_x.at[source], a_send.at[1, o], a_recv.at[1, source], 2 * o + core),
        )

    def send_b(o, which):
        return (
            remote(mine.at[1, o], got_b.at[which], b_send.at[0, o], b_recv.at[0, which], 2 * o + core),
            remote(mine_x.at[1, o], got_xb.at[which], b_send.at[1, o], b_recv.at[1, which], 2 * o + core),
        )

    which = lax.max(chip // 3 - 1, 0)
    start_sibling(0)

    @pl.when(straddles)
    def _():
        start_sibling(1)

    merge(0)
    for d in range(1, CHIPS):
        for c in send_a(lax.rem(chip + d, CHIPS), chip):
            c.start()
    got[chip] = mine[0, chip]
    got_x[chip] = mine_x[0, chip]

    @pl.when(straddles)
    def _():
        merge(1)
        for d in range(1, CHIPS):
            for c in send_b(lax.rem(chip + d, CHIPS), which):
                c.start()
        got_b[which] = mine[1, chip]
        got_xb[which] = mine_x[1, chip]

    for d in range(1, CHIPS):
        source = lax.rem(chip + d, CHIPS)
        for c in send_a(source, source):
            c.wait()
    for w, source in enumerate(STRADDLE):
        @pl.when(chip != source)
        def _():
            for c in send_b(0, w):
                c.wait_recv()

    def sums(load_a, load_b):
        fold = []
        for k in range(FOLDS):
            parts = [load_a(c) for c in range(CHIPS) if first_fold(c) == k]
            parts += [load_b(w) for w, c in enumerate(STRADDLE) if first_fold(c) == k - 1]
            fold.append(functools.reduce(lambda p, q: p + q, parts))
        total = functools.reduce(lambda p, q: p + q, fold)
        return [total - f for f in fold]

    for i in range(SLICE // 16):
        rows = slice(16 * i, 16 * i + 16)
        values = sums(lambda c: got[c, rows, :].astype(jnp.int32), lambda w: got_b[w, rows, :].astype(jnp.int32))
        for k in range(FOLDS):
            rest[k, rows, :] = values[k].astype(I16)
    values = sums(lambda c: got_x[c], lambda w: got_xb[w])
    for k in range(FOLDS):
        rest_x[k] = values[k]

    def give(k, r, source):
        target = 2 * (3 * k + r) + core
        return (
            remote(rest.at[k], gram_ref.at[source], r_send.at[0, 2 * k + r], r_recv.at[0, source], target),
            remote(rest_x.at[k], rhs_ref.at[source], r_send.at[1, 2 * k + r], r_recv.at[1, source], target),
        )

    @pl.when(jnp.logical_not(solver))
    def _():
        gram_ref[...] = jnp.zeros_like(gram_ref)
        rhs_ref[...] = jnp.zeros_like(rhs_ref)

    for k in range(FOLDS):
        for r in range(2):
            @pl.when(chip != 3 * k + r)
            def _():
                for c in give(k, r, chip):
                    c.start()

            @pl.when(chip == 3 * k + r)
            def _():
                gram_ref[chip] = rest[k]
                rhs_ref[chip] = rest_x[k]

    @pl.when(straddles)
    def _():
        for d in range(1, CHIPS):
            for c in send_b(lax.rem(chip + d, CHIPS), which):
                c.wait_send()

    for k in range(FOLDS):
        for r in range(2):
            @pl.when(chip != 3 * k + r)
            def _():
                for c in give(k, r, chip):
                    c.wait_send()

    @pl.when(solver)
    def _():
        for d in range(1, CHIPS):
            for c in give(0, 0, lax.rem(chip + d, CHIPS)):
                c.wait_recv()


def reduce_grams(part, cross):
    dma = pltpu.SemaphoreType.DMA
    return pl.pallas_call(
        reduce_kernel,
        out_shape=[
            jax.ShapeDtypeStruct((CHIPS, SLICE, 128), I16),
            jax.ShapeDtypeStruct((CHIPS, 8, 128), F32),
        ],
        in_specs=[VMEM, VMEM],
        out_specs=[VMEM, VMEM],
        scratch_shapes=[
            pltpu.VMEM((2, CHIPS * SLICE, 128), I16),
            pltpu.VMEM((2, 128, 128), F32),
            pltpu.VMEM((2, CHIPS, SLICE, 128), I16),
            pltpu.VMEM((2, CHIPS, 8, 128), F32),
            pltpu.VMEM((CHIPS, SLICE, 128), I16),
            pltpu.VMEM((CHIPS, 8, 128), F32),
            pltpu.VMEM((4, SLICE, 128), I16),
            pltpu.VMEM((4, 8, 128), F32),
            pltpu.VMEM((FOLDS, SLICE, 128), I16),
            pltpu.VMEM((FOLDS, 8, 128), F32),
            dma((4, 2)),
            dma((2, CHIPS)),
            dma((2, CHIPS)),
            dma((2, CHIPS)),
            dma((2, 4)),
            dma((2, 2 * FOLDS)),
            dma((2, CHIPS)),
        ],
        compiler_params=pltpu.CompilerParams(collective_id=0, has_side_effects=True, vmem_limit_bytes=LIMIT),
    )(part, cross)


def predict_kernel(w_ref, x_ref, out_ref, got, stacked, send, w_send, w_recv, o_send, o_recv):
    me = lax.axis_index("sample")
    group = lax.axis_index("block")
    core = lax.rem(me, 2)
    chip = me // 2
    straddles = (lax.rem(chip, 3) == 0) & (chip > 0) & (chip < 15)
    solver = (lax.rem(chip, 3) < 2) & (chip < 15)
    barrier = pltpu.get_barrier_semaphore()
    pl.semaphore_signal(barrier, inc=1, device_id={"sample": me + 1 - 2 * core}, device_id_type=MESH)
    for d in (-3, -2, -1, 1, 2, 3):
        @pl.when((chip + d >= 0) & (chip + d < CHIPS))
        def _():
            for c in range(2):
                pl.semaphore_signal(barrier, inc=1, device_id={"sample": 2 * (chip + d) + c}, device_id_type=MESH)
    for d in range(1, 8):
        pl.semaphore_signal(barrier, inc=1, device_id={"block": lax.rem(group + d, 8)}, device_id_type=MESH)
    near = lax.min(chip, 3) + lax.min(CHIPS - 1 - chip, 3)
    pl.semaphore_wait(barrier, 8 + 2 * near)

    fold = chip // 3
    ridge = lax.rem(chip, 3)

    def give(m, c):
        slot = jnp.where(fold > 0, 1, 0) if m == 0 else 0
        place = 4 * slot + 2 * core + ridge
        return remote(w_ref, got.at[place], w_send.at[m, c], w_recv.at[place], 2 * (3 * fold + m) + c)

    @pl.when(solver)
    def _():
        for m in range(4):
            for c in range(2):
                mine = (ridge == m) & (core == c)

                @pl.when(jnp.logical_not(mine))
                def _():
                    give(m, c).start()

                @pl.when(mine)
                def _():
                    slot = jnp.where(fold > 0, 1, 0) if m == 0 else 0
                    got[4 * slot + 2 * core + ridge] = w_ref[...]

    first = jnp.where(chip > 0, (chip - 1) // 3, 0)

    def receive(slot, its_fold):
        for b in range(2):
            for r in range(2):
                @pl.when(jnp.logical_not((chip == 3 * its_fold + r) & (core == b)))
                def _():
                    place = 4 * slot + 2 * b + r
                    remote(w_ref, got.at[place], w_send.at[0, 0], w_recv.at[place], me + 1 - 2 * core).wait_recv()

    to = lax.broadcasted_iota(jnp.int32, (64, 64), 0)
    source = lax.broadcasted_iota(jnp.int32, (64, 64), 1)
    swap = (source == lax.rem(to, 4) * TRAITS + to // 4).astype(BF16)
    nt = (((1,), (1,)), ((), ()))

    def product(slot):
        stacked[...] = jnp.zeros_like(stacked)
        for b in range(2):
            for r in range(2):
                at = TRAITS * (2 * b + r)
                stacked[at : at + TRAITS, WIDE * b : WIDE * b + WIDE] = got[4 * slot + 2 * b + r]
        weights = jnp.dot(swap, stacked[...], preferred_element_type=F32).astype(BF16)
        return lax.dot_general(weights, x_ref[...], nt, preferred_element_type=F32)

    receive(0, first)
    out = product(0)
    for p in range(8):
        both = jnp.concatenate([out[8 * p : 8 * p + 8, :OUT_LANES], out[8 * p : 8 * p + 8, OUT_LANES:]], axis=0)
        send[p] = both.astype(BF16)

    @pl.when(straddles)
    def _():
        receive(1, fold)
        new = product(1)
        edge = jnp.int32(0)
        for k in range(1, FOLDS):
            edge = jnp.where(fold == k, bounds()[k], edge)
        half = lax.broadcasted_iota(jnp.int32, (16, OUT_LANES), 0) // 8
        sample = me * ROWS + half * OUT_LANES + lax.broadcasted_iota(jnp.int32, (16, OUT_LANES), 1)
        for p in range(8):
            both = jnp.concatenate([new[8 * p : 8 * p + 8, :OUT_LANES], new[8 * p : 8 * p + 8, OUT_LANES:]], axis=0)
            send[p] = jnp.where(sample >= edge, both, send[p].astype(F32)).astype(BF16)

    def exchange(p, source):
        return pltpu.make_async_remote_copy(
            src_ref=send.at[p], dst_ref=out_ref.at[source], send_sem=o_send.at[p], recv_sem=o_recv.at[source],
            device_id={"block": p}, device_id_type=MESH,
        )

    for d in range(1, 8):
        exchange(lax.rem(group + d, 8), group).start()
    out_ref[group] = send[group]

    @pl.when(solver)
    def _():
        for m in range(4):
            for c in range(2):
                @pl.when(jnp.logical_not((ridge == m) & (core == c)))
                def _():
                    give(m, c).wait_send()

    for d in range(1, 8):
        peer = lax.rem(group + d, 8)
        exchange(peer, peer).wait()


def predict(weights, x):
    dma = pltpu.SemaphoreType.DMA
    return pl.pallas_call(
        predict_kernel,
        out_shape=jax.ShapeDtypeStruct((8, 16, OUT_LANES), BF16),
        in_specs=[VMEM, VMEM],
        out_specs=VMEM,
        scratch_shapes=[
            pltpu.VMEM((8, TRAITS, WIDE), BF16),
            pltpu.VMEM((4 * TRAITS, 2 * WIDE), BF16),
            pltpu.VMEM((8, 16, OUT_LANES), BF16),
            dma((4, 2)),
            dma((8,)),
            dma((8,)),
            dma((8,)),
        ],
        compiler_params=pltpu.CompilerParams(collective_id=1, has_side_effects=True, vmem_limit_bytes=LIMIT),
    )(weights, x)


def shards(genotype, allele_freq, phenotype, shrinkage, owner_order):
    me = lax.axis_index("sample")
    chip = me // 2
    core = lax.rem(me, 2)
    freq = allele_freq.reshape(2, SNPS)
    spread = jnp.sqrt(2.0 * freq * (1.0 - freq))

    def pad(value, fill):
        return jnp.pad(value, ((0, 0), (0, WIDE - SNPS)), constant_values=fill).reshape(2 * WIDE)

    zero = jnp.zeros((2 * WIDE,), F32)
    vec = jnp.stack([pad(2.0 * freq, 1.0), pad(spread, 1.0), pad(2.0 * freq - 1.0, 0.0), pad(1.0 / spread, 0.0)] + [zero] * 4)
    edge = jnp.int32(3 * ROWS)
    count = jnp.float32(1.0)
    for c in STRADDLE:
        edge = jnp.where(chip == c, bounds()[first_fold(c) + 1] - me * ROWS, edge)
    for k in range(FOLDS):
        count = jnp.where(chip // 3 == k, float(2 * ROWS * CHIPS - bounds()[k + 1] + bounds()[k]), count)
    part, cross, x = grams(edge.reshape(1), owner_order, genotype, phenotype, vec)
    gram, rhs = reduce_grams(part, cross)
    lam = jnp.where(lax.rem(chip, 3) == 1, shrinkage[1], shrinkage[0])
    own = lax.dynamic_slice_in_dim(vec, core * WIDE, WIDE, 1)
    weights = solve(jnp.stack([lam, count]), gram.reshape(CHIPS * SLICE, 128), rhs.reshape(128, 128), own)
    got = predict(weights, x)
    return jnp.transpose(got.reshape(8, 2, 2, 4, OUT_LANES), (2, 0, 3, 1, 4)).reshape(2, 32, ROWS)


def solution(mesh):
    in_specs = (P("sample", "block"), P("block"), P("sample", None), P(), P())
    out_specs = P("block", None, "sample")
    return jax.shard_map(shards, mesh=mesh, in_specs=in_specs, out_specs=out_specs, check_vma=False)
```

```python
import functools

import jax
import jax.numpy as jnp
from jax import lax
from jax.experimental import pallas as pl
from jax.experimental.pallas import tpu as pltpu
from jax.sharding import PartitionSpec as P

SNPS = 500
FOLDS = 5
WIDE = 512
ROWS = 1024
CHIPS = 16
SLICE = 64
OUT_LANES = 512
MESH = pl.DeviceIdType.MESH
BF16 = jnp.bfloat16
I16 = jnp.int16

W = 128
TRAITS = 16
PAIRS = [(i, j) for i in range(4) for j in range(i, 4)]
FULL = [(i, j) for i, j in PAIRS if i < j]
F32 = jnp.float32
HI = lax.Precision.HIGHEST


def row_of(x, i):
    return jnp.broadcast_to(x[i : i + 1, :], x.shape)


def lane_of(x, k):
    return jnp.broadcast_to(x[:, k : k + 1], x.shape)


def invert(tiles):
    sub = lax.broadcasted_iota(jnp.int32, (8, W), 0)
    lane = lax.broadcasted_iota(jnp.int32, (8, W), 1)
    for j in range(16):
        inside = (lane >= 8 * j) & (lane < 8 * j + 8)
        panel = tiles[j]
        cols = [lane_of(panel, 8 * j + i) for i in range(8)]
        rows = jnp.where(inside, (lane - 8 * j == sub).astype(F32), panel)
        for i in range(8):
            here = sub == i
            recip = 1.0 / row_of(cols[i], i)
            q = row_of(rows, i) * recip
            rows = jnp.where(here, q, rows - cols[i] * q)
            for c in range(i + 1, 8):
                qc = row_of(cols[c], i) * recip
                cols[c] = jnp.where(here, qc, cols[c] - cols[i] * qc)
        spread = [row_of(rows, i) for i in range(8)]
        new = []
        for t in range(16):
            if t == j:
                new.append(rows)
                continue
            acc = lane_of(tiles[t], 8 * j) * spread[0]
            for i in range(1, 8):
                acc = acc + lane_of(tiles[t], 8 * j + i) * spread[i]
            new.append(jnp.where(inside, 0.0, tiles[t]) - acc)
        tiles = new
    return tiles


def load_tile(ref, t):
    return jnp.concatenate([ref[2 * t], ref[2 * t + 1]], axis=0)


def load_rows(ref, t):
    return jnp.concatenate([ref[4 * t], ref[4 * t + 1]], axis=0)


def solve_part(lam, count, freq_row, gram_ref, cross_ref, out_ref, m_ref, c_ref, t_ref, d_ref):
    inv_n = 1.0 / count
    eye = lax.broadcasted_iota(jnp.int32, (W, W), 0) == lax.broadcasted_iota(jnp.int32, (W, W), 1)
    inside = lax.broadcasted_iota(jnp.int32, (1, WIDE), 1) < SNPS
    a_all = jnp.where(inside, 2.0 * freq_row - 1.0, 0.0)
    w_all = jnp.where(inside, 1.0 / jnp.sqrt(2.0 * freq_row * (1.0 - freq_row)), 0.0)
    a_row = [a_all[:, W * t : W * t + W] for t in range(4)]
    w_row = [w_all[:, W * t : W * t + W] for t in range(4)]

    def turn(row):
        return jnp.sum(jnp.where(eye, jnp.broadcast_to(row, (W, W)), 0.0), axis=1, keepdims=True)

    a_col = [turn(r) for r in a_row]
    w_col = [turn(r) for r in w_row]
    row = lax.broadcasted_iota(jnp.int32, (W, W), 0)
    lane = lax.broadcasted_iota(jnp.int32, (W, W), 1)

    def row_from(column):
        return jnp.sum(jnp.where(eye, jnp.broadcast_to(column, (W, W)), 0.0), axis=0, keepdims=True)

    sums = {p: load_tile(gram_ref, t).astype(F32) for t, p in enumerate(FULL)}
    for t in range(2):
        both = load_tile(gram_ref, 6 + t).astype(F32)
        turned = both.T
        low = pltpu.roll(both, W - 1, 0)
        if t == 0:
            low = jnp.where(row == W - 1, row_from(sums[0, 3][:, 117:118]), low)
        sums[2 * t, 2 * t] = jnp.where(row <= lane, both, turned)
        sums[2 * t + 1, 2 * t + 1] = jnp.where(row >= lane, low, low.T)
    u_col = [sums[t, 3][:, 116:117] for t in range(4)]
    v_row = [row_from(u_col[t]) - count * a_row[t] for t in range(4)]
    for i, j in PAIRS:
        s = sums[i, j]
        x = (s - u_col[i] * a_row[j] - a_col[i] * v_row[j]) * (w_col[i] * inv_n) * w_row[j]
        if i == j:
            if i == 3:
                pad = (lax.broadcasted_iota(jnp.int32, (W, W), 0) >= 116).astype(F32)
                x = x + jnp.where(eye, pad + lam, 0.0)
            else:
                x = x + jnp.where(eye, lam, 0.0)
        m_ref[i, :, W * j : W * j + W] = x
    total = load_rows(cross_ref, 3)[:, 116:117]
    for t in range(4):
        c = load_rows(cross_ref, t)
        c_ref[:, W * t : W * t + W] = (c - total * a_row[t]) * (w_row[t] * inv_n)

    dot = functools.partial(lax.dot_general, precision=HI, preferred_element_type=F32)
    nn = (((1,), (0,)), ((), ()))
    tn = (((0,), (0,)), ((), ()))
    nt = (((1,), (1,)), ((), ()))
    d_ref[...] = m_ref[0, :, 0:W]

    def step(b, carry):
        tiles = invert([d_ref[8 * t : 8 * t + 8, :] for t in range(16)])
        for t in range(16):
            d_ref[8 * t : 8 * t + 8, :] = tiles[t]
        for s in range(4):
            @pl.when(b == s)
            def _():
                dinv = d_ref[...]
                lo = W * (s + 1)
                y = dot(c_ref[:, lo - W : lo], dinv, nn)
                c_ref[:, lo - W : lo] = y
                if s < 3:
                    right = m_ref[s, :, lo:]
                    t_new = dot(dinv, right, nn)
                    t_ref[s, :, lo:] = t_new
                    c_ref[:, lo:] = c_ref[:, lo:] - dot(y, right, nn)
                    for i in range(s + 1, 4):
                        left = m_ref[s, :, W * i : W * i + W]
                        m_ref[i, :, W * i :] = m_ref[i, :, W * i :] - dot(left, t_ref[s, :, W * i :], tn)
                    d_ref[...] = m_ref[s + 1, :, lo : lo + W]
        return carry

    lax.fori_loop(0, 4, step, 0)
    for s in (2, 1, 0):
        lo = W * (s + 1)
        c_ref[:, lo - W : lo] = c_ref[:, lo - W : lo] - dot(c_ref[:, lo:], t_ref[s, :, lo:], nt)
    out_ref[...] = c_ref[...].astype(jnp.bfloat16)


VMEM = pl.BlockSpec(memory_space=pltpu.VMEM)
SMEM = pl.BlockSpec(memory_space=pltpu.SMEM)
LIMIT = 48 * 1024 * 1024


def bounds():
    return [-(-(k * ROWS * 2 * CHIPS) // FOLDS) for k in range(FOLDS + 1)]


def first_fold(chip):
    return [k for k in range(FOLDS) if bounds()[k] <= chip * 2 * ROWS < bounds()[k + 1]][0]


STRADDLE = [c for c in range(CHIPS) if bounds()[first_fold(c) + 1] < (c + 1) * 2 * ROWS]


def remote(src, dst, send, recv, sample):
    return pltpu.make_async_remote_copy(
        src_ref=src, dst_ref=dst, send_sem=send, recv_sem=recv, device_id={"sample": sample}, device_id_type=MESH
    )


def hop_from(chip, hop):
    return 8 * lax.rem(chip // 8 + hop[0], 2) + lax.rem(lax.rem(chip, 8) + hop[1] + 8, 8)


HOPS = [(x, z) for z in (4, 3, -3, 2, -2, 1, -1, 0) for x in (1, 0) if (x, z) != (0, 0)]


def reduce_part(
    barrier_wait, order_ref, geno_ref, pheno_ref, freq_ref, gram_ref, rhs_ref, x_ref,
    g_ref, y_ref, part, part_x,
    sib, sib_x, mine, mine_x, got, got_x, got_b, got_xb, rest, rest_x,
    sib_sem, a_send, a_recv, b_send, b_recv, r_send, r_recv,
):
    me = lax.axis_index("sample")
    core = lax.rem(me, 2)
    chip = me // 2
    other = me + 1 - 2 * core
    straddles = (lax.rem(chip, 3) == 0) & (chip > 0) & (chip < 15)
    solver = (lax.rem(chip, 3) < 2) & (chip < 15)

    def chip_at(hop):
        return hop_from(chip, hop)

    for b in range(2):
        for i in range(4):
            size = min(128, SNPS - 128 * i)
            at = b * SNPS + 128 * i
            g = (geno_ref[at : at + size, :] - 1).astype(F32)
            if size < 128:
                row = lax.broadcasted_iota(jnp.int32, (128 - size, ROWS), 0)
                g = jnp.concatenate([g, (row == 0).astype(F32)], axis=0)
            g_ref[b, 128 * i : 128 * i + 128, :] = g.astype(BF16)
    rows = lax.broadcasted_iota(jnp.int32, (32, TRAITS), 0)
    cols = lax.broadcasted_iota(jnp.int32, (32, TRAITS), 1)
    pick = jnp.zeros((32, TRAITS), F32)
    for q in range(TRAITS):
        pick = jnp.where((rows == q) & (cols == order_ref[q]), 1.0, pick)
    y_ref[...] = jnp.dot(pick.astype(BF16), pheno_ref[...], preferred_element_type=F32).astype(BF16)

    edge = jnp.int32(3 * ROWS)
    for c in STRADDLE:
        edge = jnp.where(chip == c, bounds()[first_fold(c) + 1], edge + 0)
    edge = jnp.where(straddles, edge - me * ROWS, 3 * ROWS)
    nt = (((1,), (1,)), ((), ()))
    eye = lax.broadcasted_iota(jnp.int32, (128, 128), 0) == lax.broadcasted_iota(jnp.int32, (128, 128), 1)
    up = lax.broadcasted_iota(jnp.int32, (128, 128), 0) <= lax.broadcasted_iota(jnp.int32, (128, 128), 1)
    lane = lax.broadcasted_iota(jnp.int32, (128, 128), 1)
    sample = lax.broadcasted_iota(jnp.int32, (128, ROWS), 1)

    def fill(b, slot):
        keep = (sample < edge) if slot == 0 else (sample >= edge)

        def times(left, right):
            left = jnp.where(keep[: left.shape[0]], left, jnp.zeros_like(left))
            return lax.dot_general(left, right, nt, preferred_element_type=F32)

        band = [times(g_ref[b, 128 * i : 128 * i + 128, :], g_ref[b, 128 * i :, :]) for i in range(4)]
        tile = {(i, j): band[i][:, 128 * (j - i) : 128 * (j - i) + 128] for i, j in PAIRS}
        tile[0, 3] = jnp.where(lane == 117, jnp.broadcast_to(tile[1, 1][:, 127:128], (128, 128)), tile[0, 3])
        packed = [tile[i, j] for i, j in FULL]
        packed += [jnp.where(up, tile[d, d], pltpu.roll(tile[d + 1, d + 1], 1, 0)) for d in (0, 2)]
        for t, value in enumerate(packed):
            part[b, slot, 128 * t : 128 * t + 128, :] = value.astype(jnp.int32).astype(I16)
        out = times(y_ref[...], g_ref[b])
        for t in range(4):
            part_x[b, slot, 32 * t : 32 * t + 32, :] = out[:, 128 * t : 128 * t + 128]

    def sibling(slot):
        return (
            remote(part.at[1 - core, slot], sib.at[slot], sib_sem.at[0, slot], sib_sem.at[1, slot], other),
            remote(part_x.at[1 - core, slot], sib_x.at[slot], sib_sem.at[2, slot], sib_sem.at[3, slot], other),
        )

    def start_sibling(slot):
        for c in sibling(slot):
            c.start()

    def merge(slot):
        for c in sibling(slot):
            c.wait()

        def add(o, carry):
            at = pl.multiple_of(o * SLICE, 16)
            left = part[core, slot, pl.ds(at, SLICE), :].astype(jnp.int32)
            right = sib[slot, pl.ds(at, SLICE), :].astype(jnp.int32)
            mine[slot, o] = (left + right).astype(I16)
            return carry

        lax.fori_loop(0, CHIPS, add, 0)
        for o in range(CHIPS):
            mine_x[slot, o] = part_x[core, slot, 8 * o : 8 * o + 8, :] + sib_x[slot, 8 * o : 8 * o + 8, :]

    def send_a(o, source):
        return (
            remote(mine.at[0, o], got.at[source], a_send.at[0, o], a_recv.at[0, source], 2 * o + core),
            remote(mine_x.at[0, o], got_x.at[source], a_send.at[1, o], a_recv.at[1, source], 2 * o + core),
        )

    def send_b(o, which):
        return (
            remote(mine.at[1, o], got_b.at[which], b_send.at[0, o], b_recv.at[0, which], 2 * o + core),
            remote(mine_x.at[1, o], got_xb.at[which], b_send.at[1, o], b_recv.at[1, which], 2 * o + core),
        )

    which = lax.max(chip // 3 - 1, 0)
    fill(1 - core, 0)
    barrier_wait()
    start_sibling(0)

    @pl.when(straddles)
    def _():
        fill(1 - core, 1)
        start_sibling(1)

    fill(core, 0)
    merge(0)
    for hop in HOPS:
        for c in send_a(chip_at(hop), chip):
            c.start()
    got[chip] = mine[0, chip]
    got_x[chip] = mine_x[0, chip]

    @pl.when(straddles)
    def _():
        fill(core, 1)
        merge(1)
        for hop in HOPS:
            for c in send_b(chip_at(hop), which):
                c.start()
        got_b[which] = mine[1, chip]
        got_xb[which] = mine_x[1, chip]

    for b in range(2):
        for i in range(4):
            size = min(128, SNPS - 128 * i)
            at = b * SNPS + 128 * i
            to = b * WIDE + 128 * i
            g = geno_ref[at : at + size, :]
            freq = jnp.broadcast_to(freq_ref[0:1, at : at + size], (size, size))
            freq = jnp.sum(jnp.where(eye[:size, :size], freq, 0.0), axis=1, keepdims=True)
            spread = jnp.sqrt(2.0 * freq * (1.0 - freq))
            zero, one, two = [(v - 2.0 * freq) / spread for v in (0.0, 1.0, 2.0)]
            x = jnp.where(g == 0, zero, jnp.where(g == 1, one, two))
            if size < 128:
                x = jnp.concatenate([x, jnp.zeros((128 - size, ROWS), F32)], axis=0)
            x_ref[to : to + 128, :] = x.astype(BF16)

    for hop in HOPS:
        source = chip_at(hop)
        for c in send_a(source, source):
            c.wait()
    for w, source in enumerate(STRADDLE):
        @pl.when(chip != source)
        def _():
            for c in send_b(0, w):
                c.wait_recv()

    def sums(load_a, load_b):
        fold = []
        for k in range(FOLDS):
            parts = [load_a(c) for c in range(CHIPS) if first_fold(c) == k]
            parts += [load_b(w) for w, c in enumerate(STRADDLE) if first_fold(c) == k - 1]
            fold.append(functools.reduce(lambda p, q: p + q, parts))
        total = functools.reduce(lambda p, q: p + q, fold)
        return [total - f for f in fold]

    for i in range(SLICE // 16):
        rows = slice(16 * i, 16 * i + 16)
        values = sums(lambda c: got[c, rows, :].astype(jnp.int32), lambda w: got_b[w, rows, :].astype(jnp.int32))
        for k in range(FOLDS):
            rest[k, rows, :] = values[k].astype(I16)
    values = sums(lambda c: got_x[c], lambda w: got_xb[w])
    for k in range(FOLDS):
        rest_x[k] = values[k]

    def give(k, r, source):
        target = 2 * (3 * k + r) + core
        return (
            remote(rest.at[k], gram_ref.at[source], r_send.at[0, 2 * k + r], r_recv.at[0, source], target),
            remote(rest_x.at[k], rhs_ref.at[source], r_send.at[1, 2 * k + r], r_recv.at[1, source], target),
        )

    for k in range(FOLDS):
        for r in range(2):
            @pl.when(chip != 3 * k + r)
            def _():
                for c in give(k, r, chip):
                    c.start()

            @pl.when(chip == 3 * k + r)
            def _():
                gram_ref[chip] = rest[k]
                rhs_ref[chip] = rest_x[k]

    @pl.when(straddles)
    def _():
        for hop in HOPS:
            for c in send_b(chip_at(hop), which):
                c.wait_send()

    for k in range(FOLDS):
        for r in range(2):
            @pl.when(chip != 3 * k + r)
            def _():
                for c in give(k, r, chip):
                    c.wait_send()

    @pl.when(solver)
    def _():
        for hop in HOPS:
            for c in give(0, 0, chip_at(hop)):
                c.wait_recv()


def predict_part(w_ref, x_ref, out_ref, got, stacked, send, w_send, w_recv, o_send, o_recv):
    me = lax.axis_index("sample")
    group = lax.axis_index("block")
    core = lax.rem(me, 2)
    chip = me // 2
    straddles = (lax.rem(chip, 3) == 0) & (chip > 0) & (chip < 15)
    solver = (lax.rem(chip, 3) < 2) & (chip < 15)
    fold = chip // 3
    ridge = lax.rem(chip, 3)

    def give(m, c):
        slot = jnp.where(fold > 0, 1, 0) if m == 0 else 0
        place = 4 * slot + 2 * core + ridge
        return remote(w_ref, got.at[place], w_send.at[m, c], w_recv.at[place], 2 * (3 * fold + m) + c)

    @pl.when(solver)
    def _():
        for m in range(4):
            for c in range(2):
                mine = (ridge == m) & (core == c)

                @pl.when(jnp.logical_not(mine))
                def _():
                    give(m, c).start()

                @pl.when(mine)
                def _():
                    slot = jnp.where(fold > 0, 1, 0) if m == 0 else 0
                    got[4 * slot + 2 * core + ridge] = w_ref[...]

    first = jnp.where(chip > 0, (chip - 1) // 3, 0)

    def receive(slot, its_fold):
        for b in range(2):
            for r in range(2):
                @pl.when(jnp.logical_not((chip == 3 * its_fold + r) & (core == b)))
                def _():
                    place = 4 * slot + 2 * b + r
                    remote(w_ref, got.at[place], w_send.at[0, 0], w_recv.at[place], me + 1 - 2 * core).wait_recv()

    to = lax.broadcasted_iota(jnp.int32, (64, 64), 0)
    source = lax.broadcasted_iota(jnp.int32, (64, 64), 1)
    swap = (source == lax.rem(to, 4) * TRAITS + to // 4).astype(BF16)

    def product(slots):
        stacked[...] = jnp.zeros_like(stacked)
        weights = []
        for slot in range(slots):
            for b in range(2):
                for r in range(2):
                    at = TRAITS * (2 * b + r)
                    stacked[at : at + TRAITS, WIDE * b : WIDE * b + WIDE] = got[4 * slot + 2 * b + r]
            weights.append(jnp.dot(swap, stacked[...], preferred_element_type=F32).astype(BF16))
        weights = jnp.concatenate(weights, axis=0)
        return jnp.dot(weights, x_ref[...], preferred_element_type=F32)

    def halves(out, p):
        return jnp.concatenate([out[8 * p : 8 * p + 8, :OUT_LANES], out[8 * p : 8 * p + 8, OUT_LANES:]], axis=0)

    receive(0, first)

    @pl.when(jnp.logical_not(straddles))
    def _():
        out = product(1)
        for p in range(8):
            send[p] = halves(out, p).astype(BF16)

    @pl.when(straddles)
    def _():
        receive(1, fold)
        out = product(2)
        edge = jnp.int32(0)
        for k in range(1, FOLDS):
            edge = jnp.where(fold == k, bounds()[k], edge)
        half = lax.broadcasted_iota(jnp.int32, (16, OUT_LANES), 0) // 8
        sample = me * ROWS + half * OUT_LANES + lax.broadcasted_iota(jnp.int32, (16, OUT_LANES), 1)
        for p in range(8):
            send[p] = jnp.where(sample >= edge, halves(out, p + 8), halves(out, p)).astype(BF16)

    def exchange(p, source):
        return pltpu.make_async_remote_copy(
            src_ref=send.at[p], dst_ref=out_ref.at[source], send_sem=o_send.at[p], recv_sem=o_recv.at[source],
            device_id={"block": p}, device_id_type=MESH,
        )

    for d in range(1, 8):
        exchange(lax.rem(group + d, 8), group).start()
    out_ref[group] = send[group]

    @pl.when(solver)
    def _():
        for m in range(4):
            for c in range(2):
                @pl.when(jnp.logical_not((ridge == m) & (core == c)))
                def _():
                    give(m, c).wait_send()

    for d in range(1, 8):
        peer = lax.rem(group + d, 8)
        exchange(peer, peer).wait()


def kernel(
    order_ref, shrink_ref, geno_ref, pheno_ref, freq_ref, out_ref,
    gram_ref, rhs_ref, x_ref, reduce_scratch, solve_scratch, w_ref, predict_scratch,
):
    me = lax.axis_index("sample")
    group = lax.axis_index("block")
    core = lax.rem(me, 2)
    chip = me // 2
    solver = (lax.rem(chip, 3) < 2) & (chip < 15)
    barrier = pltpu.get_barrier_semaphore()

    def greet(peer):
        pl.semaphore_signal(barrier, inc=1, device_id=peer, device_id_type=MESH)

    greet({"sample": me + 1 - 2 * core})
    for hop in HOPS:
        greet({"sample": 2 * hop_from(chip, hop) + core})
    for d in (-3, -2, -1, 1, 2, 3):
        @pl.when((chip + d >= 0) & (chip + d < CHIPS))
        def _():
            greet({"sample": 2 * (chip + d) + 1 - core})
    for d in range(1, 8):
        greet({"block": lax.rem(group + d, 8)})
    near = lax.min(chip, 3) + lax.min(CHIPS - 1 - chip, 3)

    def barrier_wait():
        pl.semaphore_wait(barrier, CHIPS + 7 + near)

    reduce_part(barrier_wait, order_ref, geno_ref, pheno_ref, freq_ref, gram_ref, rhs_ref, x_ref, *reduce_scratch)

    @pl.when(solver)
    def _():
        count = jnp.int32(1)
        for k in range(FOLDS):
            count = jnp.where(chip // 3 == k, 2 * ROWS * CHIPS - bounds()[k + 1] + bounds()[k], count)
        lam = jnp.where(lax.rem(chip, 3) == 1, shrink_ref[1], shrink_ref[0])
        freq = [
            jnp.concatenate([freq_ref[0:1, b * SNPS : (b + 1) * SNPS], jnp.full((1, WIDE - SNPS), 0.5, F32)], axis=1)
            for b in range(2)
        ]
        own = jnp.where(core == 0, freq[0], freq[1])
        solve_part(lam, count.astype(F32), own, gram_ref, rhs_ref, w_ref, *solve_scratch)

    predict_part(w_ref, x_ref, out_ref, *predict_scratch)


def call(order, shrinkage, geno, pheno, freq):
    dma = pltpu.SemaphoreType.DMA
    rows = CHIPS * SLICE
    return pl.pallas_call(
        kernel,
        out_shape=jax.ShapeDtypeStruct((8, 16, OUT_LANES), BF16),
        in_specs=[SMEM, SMEM, VMEM, VMEM, VMEM],
        out_specs=VMEM,
        scratch_shapes=[
            pltpu.VMEM((CHIPS, SLICE, 128), I16),
            pltpu.VMEM((CHIPS, 8, 128), F32),
            pltpu.VMEM((2 * WIDE, ROWS), BF16),
            [
                pltpu.VMEM((2, WIDE, ROWS), BF16),
                pltpu.VMEM((32, ROWS), BF16),
                pltpu.VMEM((2, 2, rows, 128), I16),
                pltpu.VMEM((2, 2, 128, 128), F32),
                pltpu.VMEM((2, rows, 128), I16),
                pltpu.VMEM((2, 128, 128), F32),
                pltpu.VMEM((2, CHIPS, SLICE, 128), I16),
                pltpu.VMEM((2, CHIPS, 8, 128), F32),
                pltpu.VMEM((CHIPS, SLICE, 128), I16),
                pltpu.VMEM((CHIPS, 8, 128), F32),
                pltpu.VMEM((4, SLICE, 128), I16),
                pltpu.VMEM((4, 8, 128), F32),
                pltpu.VMEM((FOLDS, SLICE, 128), I16),
                pltpu.VMEM((FOLDS, 8, 128), F32),
                dma((4, 2)),
                dma((2, CHIPS)),
                dma((2, CHIPS)),
                dma((2, CHIPS)),
                dma((2, 4)),
                dma((2, 2 * FOLDS)),
                dma((2, CHIPS)),
            ],
            [
                pltpu.VMEM((4, W, WIDE), F32),
                pltpu.VMEM((TRAITS, WIDE), F32),
                pltpu.VMEM((4, W, WIDE), F32),
                pltpu.VMEM((W, W), F32),
            ],
            pltpu.VMEM((TRAITS, WIDE), BF16),
            [
                pltpu.VMEM((8, TRAITS, WIDE), BF16),
                pltpu.VMEM((4 * TRAITS, 2 * WIDE), BF16),
                pltpu.VMEM((8, 16, OUT_LANES), BF16),
                dma((4, 2)),
                dma((8,)),
                dma((8,)),
                dma((8,)),
            ],
        ],
        compiler_params=pltpu.CompilerParams(collective_id=0, has_side_effects=True, vmem_limit_bytes=LIMIT),
    )(order, shrinkage, geno, pheno, freq)


def shards(genotype, allele_freq, phenotype, shrinkage, owner_order):
    got = call(owner_order, shrinkage, genotype.T, phenotype.T, allele_freq.reshape(1, 2 * SNPS))
    return jnp.transpose(got.reshape(8, 2, 2, 4, OUT_LANES), (2, 0, 3, 1, 4)).reshape(2, 32, ROWS)


def solution(mesh):
    in_specs = (P("sample", "block"), P("block"), P("sample", None), P(), P())
    out_specs = P("block", None, "sample")
    return jax.shard_map(shards, mesh=mesh, in_specs=in_specs, out_specs=out_specs, check_vma=False)
```

```python
import functools

import jax
import jax.numpy as jnp
from jax import lax
from jax.experimental import pallas as pl
from jax.experimental.pallas import tpu as pltpu
from jax.sharding import PartitionSpec as P

SNPS = 500
FOLDS = 5
WIDE = 512
ROWS = 1024
CHIPS = 16
SLICE = 64
OUT_LANES = 512
MESH = pl.DeviceIdType.MESH
BF16 = jnp.bfloat16
I16 = jnp.int16

W = 128
TRAITS = 16
PAIRS = [(i, j) for i in range(4) for j in range(i, 4)]
FULL = [(i, j) for i, j in PAIRS if i < j]
F32 = jnp.float32
HI = lax.Precision.HIGHEST


def row_of(x, i):
    return jnp.broadcast_to(x[i : i + 1, :], x.shape)


def lane_of(x, k):
    return jnp.broadcast_to(x[:, k : k + 1], x.shape)


def invert(tiles):
    sub = lax.broadcasted_iota(jnp.int32, (8, W), 0)
    lane = lax.broadcasted_iota(jnp.int32, (8, W), 1)
    for j in range(16):
        inside = (lane >= 8 * j) & (lane < 8 * j + 8)
        panel = tiles[j]
        cols = [lane_of(panel, 8 * j + i) for i in range(8)]
        rows = jnp.where(inside, (lane - 8 * j == sub).astype(F32), panel)
        for i in range(8):
            here = sub == i
            recip = 1.0 / row_of(cols[i], i)
            q = row_of(rows, i) * recip
            rows = jnp.where(here, q, rows - cols[i] * q)
            for c in range(i + 1, 8):
                qc = row_of(cols[c], i) * recip
                cols[c] = jnp.where(here, qc, cols[c] - cols[i] * qc)
        spread = [row_of(rows, i) for i in range(8)]
        turned = jnp.where(lane < 8 * j, -panel, panel)
        update = lax.dot_general(turned, rows, (((0,), (0,)), ((), ())), precision=HI, preferred_element_type=F32)
        new = []
        for t in range(16):
            if t == j:
                new.append(rows)
                continue
            if t in (j + 1, j + 2):
                acc = lane_of(tiles[t], 8 * j) * spread[0]
                for i in range(1, 8):
                    acc = acc + lane_of(tiles[t], 8 * j + i) * spread[i]
            else:
                acc = update[8 * t : 8 * t + 8, :]
            new.append(jnp.where(inside, 0.0, tiles[t]) - acc)
        tiles = new
    return tiles


def load_tile(ref, t):
    return jnp.concatenate([ref[2 * t], ref[2 * t + 1]], axis=0)


def load_rows(ref, t):
    return ref[t]


def solve_part(lam, count, freq_row, gram_ref, cross_ref, out_ref, m_ref, c_ref, t_ref, d_ref):
    inv_n = 1.0 / count
    eye = lax.broadcasted_iota(jnp.int32, (W, W), 0) == lax.broadcasted_iota(jnp.int32, (W, W), 1)
    inside = lax.broadcasted_iota(jnp.int32, (1, WIDE), 1) < SNPS
    a_all = jnp.where(inside, 2.0 * freq_row - 1.0, 0.0)
    w_all = jnp.where(inside, 1.0 / jnp.sqrt(2.0 * freq_row * (1.0 - freq_row)), 0.0)
    a_row = [a_all[:, W * t : W * t + W] for t in range(4)]
    w_row = [w_all[:, W * t : W * t + W] for t in range(4)]

    def turn(row):
        return jnp.sum(jnp.where(eye, jnp.broadcast_to(row, (W, W)), 0.0), axis=1, keepdims=True)

    a_col = [turn(r) for r in a_row]
    w_col = [turn(r) for r in w_row]
    row = lax.broadcasted_iota(jnp.int32, (W, W), 0)
    lane = lax.broadcasted_iota(jnp.int32, (W, W), 1)

    def row_from(column):
        return jnp.sum(jnp.where(eye, jnp.broadcast_to(column, (W, W)), 0.0), axis=0, keepdims=True)

    sums = {p: load_tile(gram_ref, t).astype(F32) for t, p in enumerate(FULL)}
    for t in range(2):
        both = load_tile(gram_ref, 6 + t).astype(F32)
        turned = both.T
        low = pltpu.roll(both, W - 1, 0)
        if t == 0:
            low = jnp.where(row == W - 1, row_from(sums[0, 3][:, 117:118]), low)
        sums[2 * t, 2 * t] = jnp.where(row <= lane, both, turned)
        sums[2 * t + 1, 2 * t + 1] = jnp.where(row >= lane, low, low.T)
    u_col = [sums[t, 3][:, 116:117] for t in range(4)]
    v_row = [row_from(u_col[t]) - count * a_row[t] for t in range(4)]
    for i, j in PAIRS:
        s = sums[i, j]
        x = (s - u_col[i] * a_row[j] - a_col[i] * v_row[j]) * (w_col[i] * inv_n) * w_row[j]
        if i == j:
            if i == 3:
                pad = (lax.broadcasted_iota(jnp.int32, (W, W), 0) >= 116).astype(F32)
                x = x + jnp.where(eye, pad + lam, 0.0)
            else:
                x = x + jnp.where(eye, lam, 0.0)
        m_ref[i, :, W * j : W * j + W] = x
    total = load_rows(cross_ref, 3)[:, 116:117]
    for t in range(4):
        c = load_rows(cross_ref, t)
        c_ref[:, W * t : W * t + W] = (c - total * a_row[t]) * (w_row[t] * inv_n)

    dot = functools.partial(lax.dot_general, precision=HI, preferred_element_type=F32)
    nn = (((1,), (0,)), ((), ()))
    tn = (((0,), (0,)), ((), ()))
    nt = (((1,), (1,)), ((), ()))
    d_ref[...] = m_ref[0, :, 0:W]

    def step(b, carry):
        tiles = invert([d_ref[8 * t : 8 * t + 8, :] for t in range(16)])
        for t in range(16):
            d_ref[8 * t : 8 * t + 8, :] = tiles[t]
        for s in range(4):
            @pl.when(b == s)
            def _():
                dinv = d_ref[...]
                lo = W * (s + 1)
                y = dot(c_ref[:, lo - W : lo], dinv, nn)
                c_ref[:, lo - W : lo] = y
                if s < 3:
                    right = m_ref[s, :, lo:]
                    t_new = dot(dinv, right, nn)
                    t_ref[s, :, lo:] = t_new
                    c_ref[:, lo:] = c_ref[:, lo:] - dot(y, right, nn)
                    for i in range(s + 1, 4):
                        left = m_ref[s, :, W * i : W * i + W]
                        m_ref[i, :, W * i :] = m_ref[i, :, W * i :] - dot(left, t_ref[s, :, W * i :], tn)
                    d_ref[...] = m_ref[s + 1, :, lo : lo + W]
        return carry

    lax.fori_loop(0, 4, step, 0)
    for s in (2, 1, 0):
        lo = W * (s + 1)
        c_ref[:, lo - W : lo] = c_ref[:, lo - W : lo] - dot(c_ref[:, lo:], t_ref[s, :, lo:], nt)
    out_ref[...] = c_ref[...].astype(jnp.bfloat16)


VMEM = pl.BlockSpec(memory_space=pltpu.VMEM)
HBM = pl.BlockSpec(memory_space=pltpu.HBM)
SMEM = pl.BlockSpec(memory_space=pltpu.SMEM)
LIMIT = 63 * 1024 * 1024


def bounds():
    return [-(-(k * ROWS * 2 * CHIPS) // FOLDS) for k in range(FOLDS + 1)]


def first_fold(chip):
    return [k for k in range(FOLDS) if bounds()[k] <= chip * 2 * ROWS < bounds()[k + 1]][0]


CROSS_OWNERS = (2, 5, 11, 14)
STRADDLE = [c for c in range(CHIPS) if bounds()[first_fold(c) + 1] < (c + 1) * 2 * ROWS]


def remote(src, dst, send, recv, sample):
    return pltpu.make_async_remote_copy(
        src_ref=src, dst_ref=dst, send_sem=send, recv_sem=recv, device_id={"sample": sample}, device_id_type=MESH
    )


def hop_from(chip, hop):
    return 8 * lax.rem(chip // 8 + hop[0], 2) + lax.rem(lax.rem(chip, 8) + hop[1] + 8, 8)


HOPS = [(x, z) for z in (4, 3, -3, 2, -2, 1, -1, 0) for x in (1, 0) if (x, z) != (0, 0)]


def reduce_part(
    load, settle_inputs, barrier_wait, order_ref, geno_ref, pheno_ref, freq_ref, gram_ref, rhs_ref, x_ref,
    g_ref, y_ref, part, part_x, sib, sib_x, mine, mine_x, got, got_x, rest, rest_x, sib_sem, sems,
):
    me = lax.axis_index("sample")
    core = lax.rem(me, 2)
    chip = me // 2
    other = me + 1 - 2 * core
    straddles = (lax.rem(chip, 3) == 0) & (chip > 0) & (chip < 15)
    solver = (lax.rem(chip, 3) < 2) & (chip < 15)

    def chip_at(hop):
        return hop_from(chip, hop)

    for b in range(2):
        for i in range(4):
            size = min(128, SNPS - 128 * i)
            at = b * SNPS + 128 * i
            load(at + size)
            g = (geno_ref[at : at + size, :] - 1).astype(F32)
            if size < 128:
                row = lax.broadcasted_iota(jnp.int32, (128 - size, ROWS), 0)
                g = jnp.concatenate([g, (row == 0).astype(F32)], axis=0)
            g_ref[b, 128 * i : 128 * i + 128, :] = g.astype(BF16)
    settle_inputs()
    rows = lax.broadcasted_iota(jnp.int32, (TRAITS, TRAITS), 0)
    cols = lax.broadcasted_iota(jnp.int32, (TRAITS, TRAITS), 1)
    pick = jnp.zeros((TRAITS, TRAITS), F32)
    for q in range(TRAITS):
        pick = jnp.where((rows == q) & (cols == order_ref[q]), 1.0, pick)
    y_ref[...] = jnp.dot(pick.astype(BF16), pheno_ref[...], preferred_element_type=F32).astype(BF16)

    edge = jnp.int32(3 * ROWS)
    for c in STRADDLE:
        edge = jnp.where(chip == c, bounds()[first_fold(c) + 1], edge + 0)
    edge = jnp.where(straddles, edge - me * ROWS, 3 * ROWS)
    nt = (((1,), (1,)), ((), ()))
    eye = lax.broadcasted_iota(jnp.int32, (128, 128), 0) == lax.broadcasted_iota(jnp.int32, (128, 128), 1)
    up = lax.broadcasted_iota(jnp.int32, (128, 128), 0) <= lax.broadcasted_iota(jnp.int32, (128, 128), 1)
    lane = lax.broadcasted_iota(jnp.int32, (128, 128), 1)
    sample = lax.broadcasted_iota(jnp.int32, (1, ROWS), 1)

    def fill(b, slots):
        keeps = [sample < edge, sample >= edge][:slots]
        if slots == 1:
            keeps = [sample >= 0]
        left = []
        for keep in keeps:
            for value in (g_ref[b], y_ref[...]):
                left.append(value if slots == 1 else jnp.where(keep, value, jnp.zeros_like(value)))
        height = WIDE + TRAITS
        near = [left[2 * slot][0:256] if k == 0 else left[2 * slot + 1] for slot in range(slots) for k in range(2)]
        band = [
            lax.dot_general(jnp.concatenate(near, axis=0), g_ref[b, 0:256, :], nt, preferred_element_type=F32),
            lax.dot_general(jnp.concatenate(left, axis=0), g_ref[b, 256:512, :], nt, preferred_element_type=F32),
        ]
        for slot in range(slots):
            tops = [slot * (256 + TRAITS), slot * height]

            def tile(i, j):
                at = tops[j // 2] + 128 * i
                return band[j // 2][at : at + 128, 128 * (j % 2) : 128 * (j % 2) + 128]

            spare = jnp.broadcast_to(tile(1, 1)[:, 127:128], (128, 128))
            packed = [jnp.where(lane == 117, spare, tile(i, j)) if (i, j) == (0, 3) else tile(i, j) for i, j in FULL]
            packed += [jnp.where(up, tile(d, d), pltpu.roll(tile(d + 1, d + 1), 1, 0)) for d in (0, 2)]
            for t, value in enumerate(packed):
                part[b, slot, 128 * t : 128 * t + 128, :] = value.astype(jnp.int32).astype(I16)
            for t in range(4):
                at = tops[t // 2] + (256, WIDE)[t // 2]
                part_x[b, slot, t] = band[t // 2][at : at + TRAITS, 128 * (t % 2) : 128 * (t % 2) + 128]

    def sibling(slot):
        return (
            remote(part.at[1 - core, slot], sib.at[slot], sib_sem.at[0, slot], sib_sem.at[1, slot], other),
            remote(part_x.at[1 - core, slot], sib_x.at[slot], sib_sem.at[2, slot], sib_sem.at[3, slot], other),
        )

    def start_sibling(slot):
        for c in sibling(slot):
            c.start()

    def add(o, slots):
        at = pl.multiple_of(o * SLICE, 16)
        for slot in range(slots):
            left = part[core, slot, pl.ds(at, SLICE), :].astype(jnp.int32)
            right = sib[slot, pl.ds(at, SLICE), :].astype(jnp.int32)
            mine[2 * o + slot] = (left + right).astype(I16)

    def send_gram(slots):
        for slot in range(slots):
            for c in sibling(slot):
                c.wait()
        for hop in HOPS:
            to = chip_at(hop)
            add(to, slots)
            here, there = pl.ds(2 * to, slots), pl.ds(2 * chip, slots)
            remote(mine.at[here], got.at[there], sems.at[0], sems.at[1], 2 * to + core).start()
        for t, owner in enumerate(CROSS_OWNERS):
            for slot in range(slots):
                mine_x[2 * t + slot] = part_x[core, slot, t] + sib_x[slot, t]

            @pl.when(chip != owner)
            def _():
                here, there = pl.ds(2 * t, slots), pl.ds(2 * chip, slots)
                remote(mine_x.at[here], got_x.at[there], sems.at[2], sems.at[3], 2 * owner + core).start()

            @pl.when(chip == owner)
            def _():
                for slot in range(slots):
                    got_x[2 * chip + slot] = mine_x[2 * t + slot]
        add(chip, slots)
        for slot in range(slots):
            got[2 * chip + slot] = mine[2 * chip + slot]

    def settle(array, count, sem, received):
        c = remote(array.at[pl.ds(0, count)], array.at[pl.ds(0, count)], sems.at[sem], sems.at[sem], other)
        c.wait_recv() if received else c.wait_send()

    cross_owner = (lax.rem(chip, 3) == 2) & (chip != 8)

    def local(slots):
        fill(1 - core, slots)
        barrier_wait()
        for slot in range(slots):
            start_sibling(slot)
        fill(core, slots)
        send_gram(slots)

    @pl.when(jnp.logical_not(straddles))
    def _():
        local(1)

    @pl.when(straddles)
    def _():
        local(2)

    for b in range(2):
        for i in range(4):
            size = min(128, SNPS - 128 * i)
            at = b * SNPS + 128 * i
            to = b * WIDE + 128 * i
            g = geno_ref[at : at + size, :]
            freq = jnp.broadcast_to(freq_ref[0:1, at : at + size], (size, size))
            freq = jnp.sum(jnp.where(eye[:size, :size], freq, 0.0), axis=1, keepdims=True)
            spread = jnp.sqrt(2.0 * freq * (1.0 - freq))
            zero, one, two = [(v - 2.0 * freq) / spread for v in (0.0, 1.0, 2.0)]
            x = jnp.where(g == 0, zero, jnp.where(g == 1, one, two))
            if size < 128:
                x = jnp.concatenate([x, jnp.zeros((128 - size, ROWS), F32)], axis=0)
            x_ref[to : to + 128, :] = x.astype(BF16)

    @pl.when(straddles)
    def _():
        settle(got, 18, 1, True)

    @pl.when(jnp.logical_not(straddles))
    def _():
        settle(got, 19, 1, True)

    def sums(load_a, load_b):
        fold = []
        for k in range(FOLDS):
            parts = [load_a(c) for c in range(CHIPS) if first_fold(c) == k]
            parts += [load_b(w) for w, c in enumerate(STRADDLE) if first_fold(c) == k - 1]
            fold.append(functools.reduce(lambda p, q: p + q, parts))
        total = functools.reduce(lambda p, q: p + q, fold)
        return [total - f for f in fold]

    for i in range(SLICE // 16):
        rows = slice(16 * i, 16 * i + 16)
        values = sums(
            lambda c: got[2 * c, rows, :].astype(jnp.int32), lambda w: got[2 * STRADDLE[w] + 1, rows, :].astype(jnp.int32)
        )
        for k in range(FOLDS):
            rest[k, rows, :] = values[k].astype(I16)

    for k in range(FOLDS):
        for r in range(2):
            @pl.when(chip != 3 * k + r)
            def _():
                remote(rest.at[k], gram_ref.at[chip], sems.at[4], sems.at[5], 2 * (3 * k + r) + core).start()

            @pl.when(chip == 3 * k + r)
            def _():
                gram_ref[chip] = rest[k]

    @pl.when(cross_owner)
    def _():
        settle(got_x, 19, 3, True)
        values = sums(lambda c: got_x[2 * c], lambda w: got_x[2 * STRADDLE[w] + 1])
        for k in range(FOLDS):
            rest_x[k] = values[k]
        place = (chip - 2) // 3 - jnp.where(chip > 8, 1, 0)
        for k in range(FOLDS):
            for r in range(2):
                remote(rest_x.at[k], rhs_ref.at[place], sems.at[6], sems.at[7], 2 * (3 * k + r) + core).start()

    @pl.when(straddles)
    def _():
        settle(got, 30, 0, False)
        settle(got_x, 8, 2, False)

    @pl.when(jnp.logical_not(straddles))
    def _():
        settle(got, 15, 0, False)

        @pl.when(cross_owner)
        def _():
            settle(got_x, 3, 2, False)

        @pl.when(jnp.logical_not(cross_owner))
        def _():
            settle(got_x, 4, 2, False)

    @pl.when(solver)
    def _():
        settle(got, 15, 5, True)
        settle(got_x, 4, 7, True)

    def finish():
        @pl.when(solver)
        def _():
            settle(got, 9, 4, False)

        @pl.when(jnp.logical_not(solver))
        def _():
            settle(got, 10, 4, False)

        @pl.when(cross_owner)
        def _():
            settle(got_x, 10, 6, False)

    finish()


def predict_part(w_ref, x_ref, out_ref, got, stacked, send, landed, sems):
    me = lax.axis_index("sample")
    group = lax.axis_index("block")
    core = lax.rem(me, 2)
    chip = me // 2
    straddles = (lax.rem(chip, 3) == 0) & (chip > 0) & (chip < 15)
    solver = (lax.rem(chip, 3) < 2) & (chip < 15)
    fold = chip // 3
    ridge = lax.rem(chip, 3)

    def give(m, c):
        slot = jnp.where(fold > 0, 1, 0) if m == 0 else 0
        place = 4 * slot + 2 * core + ridge
        return remote(w_ref, got.at[place], sems.at[0], sems.at[1], 2 * (3 * fold + m) + c)

    @pl.when(solver)
    def _():
        for m in range(4):
            for c in range(2):
                mine = (ridge == m) & (core == c)

                @pl.when(jnp.logical_not(mine))
                def _():
                    give(m, c).start()

                @pl.when(mine)
                def _():
                    slot = jnp.where(fold > 0, 1, 0) if m == 0 else 0
                    got[4 * slot + 2 * core + ridge] = w_ref[...]

    def settle(array, count, sem, received):
        c = remote(array.at[pl.ds(0, count)], array.at[pl.ds(0, count)], sems.at[sem], sems.at[sem], me + 1 - 2 * core)
        c.wait_recv() if received else c.wait_send()

    def product(slots):
        for slot in range(slots):
            for b in range(2):
                for r in range(2):
                    value = got[4 * slot + 2 * b + r].astype(F32)
                    rows = pl.ds(64 * slot + 2 * b + r, TRAITS, stride=4)
                    for t in range(4):
                        stacked[4 * b + t, rows, :] = value[:, 128 * t : 128 * t + 128]
        weights = jnp.concatenate([stacked[t, 0 : 64 * slots, :].astype(BF16) for t in range(8)], axis=1)
        return jnp.dot(weights, x_ref[...], preferred_element_type=F32)

    def halves(out, p):
        return jnp.concatenate([out[8 * p : 8 * p + 8, :OUT_LANES], out[8 * p : 8 * p + 8, OUT_LANES:]], axis=0)

    @pl.when(jnp.logical_not(straddles))
    def _():
        @pl.when(solver)
        def _():
            settle(got, 3, 1, True)

        @pl.when(jnp.logical_not(solver))
        def _():
            settle(got, 4, 1, True)

        out = product(1)
        for p in range(8):
            send[p] = halves(out, p).astype(BF16)

    @pl.when(straddles)
    def _():
        settle(got, 7, 1, True)
        out = product(2)
        edge = jnp.int32(0)
        for k in range(1, FOLDS):
            edge = jnp.where(fold == k, bounds()[k], edge)
        half = lax.broadcasted_iota(jnp.int32, (16, OUT_LANES), 0) // 8
        sample = me * ROWS + half * OUT_LANES + lax.broadcasted_iota(jnp.int32, (16, OUT_LANES), 1)
        for p in range(8):
            send[p] = jnp.where(sample >= edge, halves(out, p + 8), halves(out, p)).astype(BF16)

    for d in range(1, 8):
        peer = lax.rem(group + d, 8)
        pltpu.make_async_remote_copy(
            src_ref=send.at[peer], dst_ref=landed.at[group], send_sem=sems.at[2], recv_sem=sems.at[3],
            device_id={"block": peer}, device_id_type=MESH,
        ).start()
    landed[group] = send[group]

    @pl.when(solver)
    def _():
        settle(got, 7, 0, False)

    settle(send, 7, 3, True)
    low = lax.broadcasted_iota(jnp.int32, (8, OUT_LANES), 0) < 4
    for half in range(2):
        value = [landed[p].astype(F32)[8 * half : 8 * half + 8] for p in range(8)]
        for q in range(2):
            tiles = []
            for p in range(0, 8, 2):
                if q == 0:
                    tiles.append(jnp.where(low, value[p], pltpu.roll(value[p + 1], 4, 0)))
                else:
                    tiles.append(jnp.where(low, pltpu.roll(value[p], 4, 0), value[p + 1]))
            out_ref[q, :, OUT_LANES * half : OUT_LANES * (half + 1)] = jnp.concatenate(tiles, axis=0).astype(BF16)
    settle(send, 7, 2, False)


def kernel(
    order_ref, shrink_ref, geno_hbm, pheno_hbm, freq_hbm, out_ref, geno_ref, pheno_ref, freq_ref, in_sem,
    gram_ref, rhs_ref, x_ref, reduce_scratch, solve_scratch, w_ref, predict_scratch,
):
    snps = geno_hbm.shape[0]
    chunks = [slice(at, min(at + 128, snps)) for at in range(0, snps, 128)]
    copies = [pltpu.make_async_copy(geno_hbm.at[c, :], geno_ref.at[c, :], in_sem.at[i]) for i, c in enumerate(chunks)]
    copies += [
        pltpu.make_async_copy(freq_hbm, freq_ref, in_sem.at[8]),
        pltpu.make_async_copy(pheno_hbm, pheno_ref, in_sem.at[9]),
    ]
    for c in copies:
        c.start()
    loaded = [0]

    def load(end):
        while loaded[0] * 128 < end:
            copies[loaded[0]].wait()
            loaded[0] += 1

    me = lax.axis_index("sample")
    group = lax.axis_index("block")
    core = lax.rem(me, 2)
    chip = me // 2
    solver = (lax.rem(chip, 3) < 2) & (chip < 15)
    barrier = pltpu.get_barrier_semaphore()

    def greet(peer):
        pl.semaphore_signal(barrier, inc=1, device_id=peer, device_id_type=MESH)

    greet({"sample": me + 1 - 2 * core})
    for hop in HOPS:
        greet({"sample": 2 * hop_from(chip, hop) + core})
    for d in (-3, -2, -1, 1, 2, 3):
        @pl.when((chip + d >= 0) & (chip + d < CHIPS))
        def _():
            greet({"sample": 2 * (chip + d) + 1 - core})
    for d in range(1, 8):
        greet({"block": lax.rem(group + d, 8)})
    near = lax.min(chip, 3) + lax.min(CHIPS - 1 - chip, 3)

    def barrier_wait():
        pl.semaphore_wait(barrier, CHIPS + 7 + near)

    def settle_inputs():
        copies[8].wait()
        copies[9].wait()

    predict_scratch[1][...] = jnp.zeros_like(predict_scratch[1])
    reduce_part(load, settle_inputs, barrier_wait, order_ref, geno_ref, pheno_ref, freq_ref, gram_ref, rhs_ref, x_ref, *reduce_scratch)

    @pl.when(solver)
    def _():
        count = jnp.int32(1)
        for k in range(FOLDS):
            count = jnp.where(chip // 3 == k, 2 * ROWS * CHIPS - bounds()[k + 1] + bounds()[k], count)
        lam = jnp.where(lax.rem(chip, 3) == 1, shrink_ref[1], shrink_ref[0])
        freq = [
            jnp.concatenate([freq_ref[0:1, b * SNPS : (b + 1) * SNPS], jnp.full((1, WIDE - SNPS), 0.5, F32)], axis=1)
            for b in range(2)
        ]
        own = jnp.where(core == 0, freq[0], freq[1])
        solve_part(lam, count.astype(F32), own, gram_ref, rhs_ref, w_ref, *solve_scratch)

    predict_part(w_ref, x_ref, out_ref, *predict_scratch)


def call(order, shrinkage, geno, pheno, freq):
    dma = pltpu.SemaphoreType.DMA
    rows = CHIPS * SLICE
    return pl.pallas_call(
        kernel,
        out_shape=jax.ShapeDtypeStruct((2, 32, ROWS), BF16),
        in_specs=[SMEM, SMEM, HBM, HBM, HBM],
        out_specs=VMEM,
        scratch_shapes=[
            pltpu.VMEM((2 * SNPS, ROWS), jnp.int32),
            pltpu.VMEM((TRAITS, ROWS), BF16),
            pltpu.VMEM((1, 2 * SNPS), F32),
            dma((10,)),
            pltpu.VMEM((CHIPS, SLICE, 128), I16),
            pltpu.VMEM((4, TRAITS, 128), F32),
            pltpu.VMEM((2 * WIDE, ROWS), BF16),
            [
                pltpu.VMEM((2, WIDE, ROWS), BF16),
                pltpu.VMEM((TRAITS, ROWS), BF16),
                pltpu.VMEM((2, 2, rows, 128), I16),
                pltpu.VMEM((2, 2, 4, TRAITS, 128), F32),
                pltpu.VMEM((2, rows, 128), I16),
                pltpu.VMEM((2, 4, TRAITS, 128), F32),
                pltpu.VMEM((2 * CHIPS, SLICE, 128), I16),
                pltpu.VMEM((8, TRAITS, 128), F32),
                pltpu.VMEM((2 * CHIPS, SLICE, 128), I16),
                pltpu.VMEM((2 * CHIPS, TRAITS, 128), F32),
                pltpu.VMEM((FOLDS, SLICE, 128), I16),
                pltpu.VMEM((FOLDS, TRAITS, 128), F32),
                dma((4, 2)),
                dma((8,)),
            ],
            [
                pltpu.VMEM((4, W, WIDE), F32),
                pltpu.VMEM((TRAITS, WIDE), F32),
                pltpu.VMEM((4, W, WIDE), F32),
                pltpu.VMEM((W, W), F32),
            ],
            pltpu.VMEM((TRAITS, WIDE), BF16),
            [
                pltpu.VMEM((8, TRAITS, WIDE), BF16),
                pltpu.VMEM((8, 8 * TRAITS, 128), F32),
                pltpu.VMEM((8, 16, OUT_LANES), BF16),
                pltpu.VMEM((8, 16, OUT_LANES), BF16),
                dma((4,)),
            ],
        ],
        compiler_params=pltpu.CompilerParams(collective_id=0, has_side_effects=True, vmem_limit_bytes=LIMIT),
    )(order, shrinkage, geno, pheno, freq)


def shards(genotype, allele_freq, phenotype, shrinkage, owner_order):
    return call(owner_order, shrinkage, genotype.T, phenotype.T, allele_freq.reshape(1, 2 * SNPS))


def solution(mesh):
    in_specs = (P("sample", "block"), P("block"), P("sample", None), P(), P())
    out_specs = P("block", None, "sample")
    return jax.shard_map(shards, mesh=mesh, in_specs=in_specs, out_specs=out_specs, check_vma=False)
```

```python
import functools

import jax
import jax.numpy as jnp
from jax import lax
from jax.experimental import pallas as pl
from jax.experimental.pallas import tpu as pltpu
from jax.sharding import PartitionSpec as P

SNPS = 500
FOLDS = 5
WIDE = 512
ROWS = 1024
CHIPS = 16
SLICE = 64
OUT_LANES = 512
MESH = pl.DeviceIdType.MESH
BF16 = jnp.bfloat16
I16 = jnp.int16

W = 128
TRAITS = 16
PAIRS = [(i, j) for i in range(4) for j in range(i, 4)]
FULL = [(i, j) for i, j in PAIRS if i < j]
F32 = jnp.float32
HI = lax.Precision.HIGHEST


def row_of(x, i):
    return jnp.broadcast_to(x[i : i + 1, :], x.shape)


def lane_of(x, k):
    return jnp.broadcast_to(x[:, k : k + 1], x.shape)


def invert(tiles):
    sub = lax.broadcasted_iota(jnp.int32, (8, W), 0)
    lane = lax.broadcasted_iota(jnp.int32, (8, W), 1)
    for j in range(16):
        inside = (lane >= 8 * j) & (lane < 8 * j + 8)
        panel = tiles[j]
        cols = [lane_of(panel, 8 * j + i) for i in range(8)]
        rows = jnp.where(inside, (lane - 8 * j == sub).astype(F32), panel)
        for i in range(8):
            here = sub == i
            recip = 1.0 / row_of(cols[i], i)
            q = row_of(rows, i) * recip
            rows = jnp.where(here, q, rows - cols[i] * q)
            for c in range(i + 1, 8):
                qc = row_of(cols[c], i) * recip
                cols[c] = jnp.where(here, qc, cols[c] - cols[i] * qc)
        spread = [row_of(rows, i) for i in range(8)]
        turned = jnp.where(lane < 8 * j, -panel, panel)
        update = lax.dot_general(turned, rows, (((0,), (0,)), ((), ())), precision=HI, preferred_element_type=F32)
        new = []
        for t in range(16):
            if t == j:
                new.append(rows)
                continue
            if t in (j + 1, j + 2):
                acc = lane_of(tiles[t], 8 * j) * spread[0]
                for i in range(1, 8):
                    acc = acc + lane_of(tiles[t], 8 * j + i) * spread[i]
            else:
                acc = update[8 * t : 8 * t + 8, :]
            new.append(jnp.where(inside, 0.0, tiles[t]) - acc)
        tiles = new
    return tiles


def load_tile(ref, t):
    return jnp.concatenate([ref[2 * t], ref[2 * t + 1]], axis=0)


def load_rows(ref, t):
    return ref[t]


def solve_part(lam, count, freq_row, gram_ref, cross_ref, out_ref, m_ref, c_ref, t_ref, d_ref):
    inv_n = 1.0 / count
    eye = lax.broadcasted_iota(jnp.int32, (W, W), 0) == lax.broadcasted_iota(jnp.int32, (W, W), 1)
    inside = lax.broadcasted_iota(jnp.int32, (1, WIDE), 1) < SNPS
    a_all = jnp.where(inside, 2.0 * freq_row - 1.0, 0.0)
    w_all = jnp.where(inside, 1.0 / jnp.sqrt(2.0 * freq_row * (1.0 - freq_row)), 0.0)
    a_row = [a_all[:, W * t : W * t + W] for t in range(4)]
    w_row = [w_all[:, W * t : W * t + W] for t in range(4)]

    def turn(row):
        return jnp.sum(jnp.where(eye, jnp.broadcast_to(row, (W, W)), 0.0), axis=1, keepdims=True)

    a_col = [turn(r) for r in a_row]
    w_col = [turn(r) for r in w_row]
    row = lax.broadcasted_iota(jnp.int32, (W, W), 0)
    lane = lax.broadcasted_iota(jnp.int32, (W, W), 1)

    def row_from(column):
        return jnp.sum(jnp.where(eye, jnp.broadcast_to(column, (W, W)), 0.0), axis=0, keepdims=True)

    sums = {p: load_tile(gram_ref, t).astype(F32) for t, p in enumerate(FULL)}
    for t in range(2):
        both = load_tile(gram_ref, 6 + t).astype(F32)
        turned = both.T
        low = pltpu.roll(both, W - 1, 0)
        if t == 0:
            low = jnp.where(row == W - 1, row_from(sums[0, 3][:, 117:118]), low)
        sums[2 * t, 2 * t] = jnp.where(row <= lane, both, turned)
        sums[2 * t + 1, 2 * t + 1] = jnp.where(row >= lane, low, low.T)
    u_col = [sums[t, 3][:, 116:117] for t in range(4)]
    v_row = [row_from(u_col[t]) - count * a_row[t] for t in range(4)]
    for i, j in PAIRS:
        s = sums[i, j]
        x = (s - u_col[i] * a_row[j] - a_col[i] * v_row[j]) * (w_col[i] * inv_n) * w_row[j]
        if i == j:
            if i == 3:
                pad = (lax.broadcasted_iota(jnp.int32, (W, W), 0) >= 116).astype(F32)
                x = x + jnp.where(eye, pad + lam, 0.0)
            else:
                x = x + jnp.where(eye, lam, 0.0)
        m_ref[i, :, W * j : W * j + W] = x
    total = load_rows(cross_ref, 3)[:, 116:117]
    for t in range(4):
        c = load_rows(cross_ref, t)
        c_ref[:, W * t : W * t + W] = (c - total * a_row[t]) * (w_row[t] * inv_n)

    dot = functools.partial(lax.dot_general, precision=HI, preferred_element_type=F32)
    nn = (((1,), (0,)), ((), ()))
    tn = (((0,), (0,)), ((), ()))
    nt = (((1,), (1,)), ((), ()))
    d_ref[...] = m_ref[0, :, 0:W]

    def step(b, carry):
        tiles = invert([d_ref[8 * t : 8 * t + 8, :] for t in range(16)])
        for t in range(16):
            d_ref[8 * t : 8 * t + 8, :] = tiles[t]
        for s in range(4):
            @pl.when(b == s)
            def _():
                dinv = d_ref[...]
                lo = W * (s + 1)
                y = dot(c_ref[:, lo - W : lo], dinv, nn)
                c_ref[:, lo - W : lo] = y
                if s < 3:
                    right = m_ref[s, :, lo:]
                    t_new = dot(dinv, right, nn)
                    t_ref[s, :, lo:] = t_new
                    c_ref[:, lo:] = c_ref[:, lo:] - dot(y, right, nn)
                    for i in range(s + 1, 4):
                        left = m_ref[s, :, W * i : W * i + W]
                        m_ref[i, :, W * i :] = m_ref[i, :, W * i :] - dot(left, t_ref[s, :, W * i :], tn)
                    d_ref[...] = m_ref[s + 1, :, lo : lo + W]
        return carry

    lax.fori_loop(0, 4, step, 0)
    for s in (2, 1, 0):
        lo = W * (s + 1)
        c_ref[:, lo - W : lo] = c_ref[:, lo - W : lo] - dot(c_ref[:, lo:], t_ref[s, :, lo:], nt)
    out_ref[...] = c_ref[...].astype(jnp.bfloat16)


VMEM = pl.BlockSpec(memory_space=pltpu.VMEM)
HBM = pl.BlockSpec(memory_space=pltpu.HBM)
SMEM = pl.BlockSpec(memory_space=pltpu.SMEM)
LIMIT = 63 * 1024 * 1024


def bounds():
    return [-(-(k * ROWS * 2 * CHIPS) // FOLDS) for k in range(FOLDS + 1)]


def first_fold(chip):
    return [k for k in range(FOLDS) if bounds()[k] <= chip * 2 * ROWS < bounds()[k + 1]][0]


CROSS_OWNERS = (2, 5, 11, 14)
STRADDLE = [c for c in range(CHIPS) if bounds()[first_fold(c) + 1] < (c + 1) * 2 * ROWS]


def remote(src, dst, send, recv, sample):
    return pltpu.make_async_remote_copy(
        src_ref=src, dst_ref=dst, send_sem=send, recv_sem=recv, device_id={"sample": sample}, device_id_type=MESH
    )


def hop_from(chip, hop):
    return 8 * lax.rem(chip // 8 + hop[0], 2) + lax.rem(lax.rem(chip, 8) + hop[1] + 8, 8)


HOPS = [(x, z) for z in (4, 3, -3, 2, -2, 1, -1, 0) for x in (1, 0) if (x, z) != (0, 0)]


def reduce_part(
    load, settle_inputs, barrier_wait, order_ref, geno_ref, pheno_ref, freq_ref, gram_ref, rhs_ref, x_ref,
    g_ref, y_ref, part, part_x, sib, sib_x, mine, mine_x, got, got_x, rest, rest_x, sib_sem, sems,
):
    me = lax.axis_index("sample")
    core = lax.rem(me, 2)
    chip = me // 2
    other = me + 1 - 2 * core
    straddles = (lax.rem(chip, 3) == 0) & (chip > 0) & (chip < 15)
    solver = (lax.rem(chip, 3) < 2) & (chip < 15)

    def chip_at(hop):
        return hop_from(chip, hop)

    for b in range(2):
        for i in range(4):
            size = min(128, SNPS - 128 * i)
            at = b * SNPS + 128 * i
            load(at + size)
            g = (geno_ref[at : at + size, :] - 1).astype(F32)
            if size < 128:
                row = lax.broadcasted_iota(jnp.int32, (128 - size, ROWS), 0)
                g = jnp.concatenate([g, (row == 0).astype(F32)], axis=0)
            g_ref[b, 128 * i : 128 * i + 128, :] = g.astype(BF16)
    settle_inputs()
    rows = lax.broadcasted_iota(jnp.int32, (TRAITS, TRAITS), 0)
    cols = lax.broadcasted_iota(jnp.int32, (TRAITS, TRAITS), 1)
    pick = jnp.zeros((TRAITS, TRAITS), F32)
    for q in range(TRAITS):
        pick = jnp.where((rows == q) & (cols == order_ref[q]), 1.0, pick)
    y_ref[...] = jnp.dot(pick.astype(BF16), pheno_ref[...], preferred_element_type=F32).astype(BF16)

    edge = jnp.int32(3 * ROWS)
    for c in STRADDLE:
        edge = jnp.where(chip == c, bounds()[first_fold(c) + 1], edge + 0)
    edge = jnp.where(straddles, edge - me * ROWS, 3 * ROWS)
    nt = (((1,), (1,)), ((), ()))
    eye = lax.broadcasted_iota(jnp.int32, (128, 128), 0) == lax.broadcasted_iota(jnp.int32, (128, 128), 1)
    up = lax.broadcasted_iota(jnp.int32, (128, 128), 0) <= lax.broadcasted_iota(jnp.int32, (128, 128), 1)
    lane = lax.broadcasted_iota(jnp.int32, (128, 128), 1)
    sample = lax.broadcasted_iota(jnp.int32, (1, ROWS), 1)

    def fill(b, slots):
        keeps = [sample < edge, sample >= edge][:slots]
        if slots == 1:
            keeps = [sample >= 0]
        left = []
        for keep in keeps:
            for value in (g_ref[b], y_ref[...]):
                left.append(value if slots == 1 else jnp.where(keep, value, jnp.zeros_like(value)))
        height = WIDE + TRAITS
        near = [left[2 * slot][0:256] if k == 0 else left[2 * slot + 1] for slot in range(slots) for k in range(2)]
        band = [
            lax.dot_general(jnp.concatenate(near, axis=0), g_ref[b, 0:256, :], nt, preferred_element_type=F32),
            lax.dot_general(jnp.concatenate(left, axis=0), g_ref[b, 256:512, :], nt, preferred_element_type=F32),
        ]
        for slot in range(slots):
            tops = [slot * (256 + TRAITS), slot * height]

            def tile(i, j):
                at = tops[j // 2] + 128 * i
                return band[j // 2][at : at + 128, 128 * (j % 2) : 128 * (j % 2) + 128]

            spare = jnp.broadcast_to(tile(1, 1)[:, 127:128], (128, 128))
            packed = [jnp.where(lane == 117, spare, tile(i, j)) if (i, j) == (0, 3) else tile(i, j) for i, j in FULL]
            packed += [jnp.where(up, tile(d, d), pltpu.roll(tile(d + 1, d + 1), 1, 0)) for d in (0, 2)]
            for t, value in enumerate(packed):
                part[b, slot, 128 * t : 128 * t + 128, :] = value.astype(jnp.int32).astype(I16)
            for t in range(4):
                at = tops[t // 2] + (256, WIDE)[t // 2]
                part_x[b, slot, t] = band[t // 2][at : at + TRAITS, 128 * (t % 2) : 128 * (t % 2) + 128]

    def sibling(slot):
        return (
            remote(part.at[1 - core, slot], sib.at[slot], sib_sem.at[0, slot], sib_sem.at[1, slot], other),
            remote(part_x.at[1 - core, slot], sib_x.at[slot], sib_sem.at[2, slot], sib_sem.at[3, slot], other),
        )

    def start_sibling(slot):
        for c in sibling(slot):
            c.start()

    def add(o, slots):
        at = pl.multiple_of(o * SLICE, 16)
        for slot in range(slots):
            left = part[core, slot, pl.ds(at, SLICE), :].astype(jnp.int32)
            right = sib[slot, pl.ds(at, SLICE), :].astype(jnp.int32)
            mine[2 * o + slot] = (left + right).astype(I16)

    def send_gram(slots):
        for slot in range(slots):
            for c in sibling(slot):
                c.wait()
        for hop in HOPS:
            to = chip_at(hop)
            add(to, slots)
            here, there = pl.ds(2 * to, slots), pl.ds(2 * chip, slots)
            remote(mine.at[here], got.at[there], sems.at[0], sems.at[1], 2 * to + core).start()
        for t, owner in enumerate(CROSS_OWNERS):
            for slot in range(slots):
                mine_x[2 * t + slot] = part_x[core, slot, t] + sib_x[slot, t]

            @pl.when(chip != owner)
            def _():
                here, there = pl.ds(2 * t, slots), pl.ds(2 * chip, slots)
                remote(mine_x.at[here], got_x.at[there], sems.at[2], sems.at[3], 2 * owner + core).start()

            @pl.when(chip == owner)
            def _():
                for slot in range(slots):
                    got_x[2 * chip + slot] = mine_x[2 * t + slot]
        add(chip, slots)
        for slot in range(slots):
            got[2 * chip + slot] = mine[2 * chip + slot]

    def settle(array, count, sem, received):
        c = remote(array.at[pl.ds(0, count)], array.at[pl.ds(0, count)], sems.at[sem], sems.at[sem], other)
        c.wait_recv() if received else c.wait_send()

    cross_owner = (lax.rem(chip, 3) == 2) & (chip != 8)

    def local(slots):
        fill(1 - core, slots)
        barrier_wait()
        for slot in range(slots):
            start_sibling(slot)
        fill(core, slots)
        send_gram(slots)

    @pl.when(jnp.logical_not(straddles))
    def _():
        local(1)

    @pl.when(straddles)
    def _():
        local(2)

    for b in range(2):
        for i in range(4):
            size = min(128, SNPS - 128 * i)
            at = b * SNPS + 128 * i
            to = b * WIDE + 128 * i
            g = geno_ref[at : at + size, :]
            freq = jnp.broadcast_to(freq_ref[0:1, at : at + size], (size, size))
            freq = jnp.sum(jnp.where(eye[:size, :size], freq, 0.0), axis=1, keepdims=True)
            spread = jnp.sqrt(2.0 * freq * (1.0 - freq))
            zero, one, two = [(v - 2.0 * freq) / spread for v in (0.0, 1.0, 2.0)]
            x = jnp.where(g == 0, zero, jnp.where(g == 1, one, two))
            if size < 128:
                x = jnp.concatenate([x, jnp.zeros((128 - size, ROWS), F32)], axis=0)
            x_ref[to : to + 128, :] = x.astype(BF16)

    @pl.when(straddles)
    def _():
        settle(got, 18, 1, True)

    @pl.when(jnp.logical_not(straddles))
    def _():
        settle(got, 19, 1, True)

    def sums(load_a, load_b):
        fold = []
        for k in range(FOLDS):
            parts = [load_a(c) for c in range(CHIPS) if first_fold(c) == k]
            parts += [load_b(w) for w, c in enumerate(STRADDLE) if first_fold(c) == k - 1]
            fold.append(functools.reduce(lambda p, q: p + q, parts))
        total = functools.reduce(lambda p, q: p + q, fold)
        return [total - f for f in fold]

    for i in range(SLICE // 16):
        rows = slice(16 * i, 16 * i + 16)
        values = sums(
            lambda c: got[2 * c, rows, :].astype(jnp.int32), lambda w: got[2 * STRADDLE[w] + 1, rows, :].astype(jnp.int32)
        )
        for k in range(FOLDS):
            rest[k, rows, :] = values[k].astype(I16)

    for k in range(FOLDS):
        for r in range(2):
            @pl.when(chip != 3 * k + r)
            def _():
                remote(rest.at[k], gram_ref.at[chip], sems.at[4], sems.at[5], 2 * (3 * k + r) + core).start()

            @pl.when(chip == 3 * k + r)
            def _():
                gram_ref[chip] = rest[k]

    @pl.when(cross_owner)
    def _():
        settle(got_x, 19, 3, True)
        values = sums(lambda c: got_x[2 * c], lambda w: got_x[2 * STRADDLE[w] + 1])
        for k in range(FOLDS):
            rest_x[k] = values[k]
        place = (chip - 2) // 3 - jnp.where(chip > 8, 1, 0)
        for k in range(FOLDS):
            for r in range(2):
                remote(rest_x.at[k], rhs_ref.at[place], sems.at[6], sems.at[7], 2 * (3 * k + r) + core).start()

    @pl.when(straddles)
    def _():
        settle(got, 30, 0, False)
        settle(got_x, 8, 2, False)

    @pl.when(jnp.logical_not(straddles))
    def _():
        settle(got, 15, 0, False)

        @pl.when(cross_owner)
        def _():
            settle(got_x, 3, 2, False)

        @pl.when(jnp.logical_not(cross_owner))
        def _():
            settle(got_x, 4, 2, False)

    @pl.when(solver)
    def _():
        settle(got, 15, 5, True)
        settle(got_x, 4, 7, True)

    def finish():
        @pl.when(solver)
        def _():
            settle(got, 9, 4, False)

        @pl.when(jnp.logical_not(solver))
        def _():
            settle(got, 10, 4, False)

        @pl.when(cross_owner)
        def _():
            settle(got_x, 10, 6, False)

    finish()


def predict_part(w_ref, x_ref, out_ref, got, stacked, send, landed, sems):
    me = lax.axis_index("sample")
    group = lax.axis_index("block")
    core = lax.rem(me, 2)
    chip = me // 2
    straddles = (lax.rem(chip, 3) == 0) & (chip > 0) & (chip < 15)
    solver = (lax.rem(chip, 3) < 2) & (chip < 15)
    fold = chip // 3
    ridge = lax.rem(chip, 3)

    def give(m, c):
        slot = jnp.where(fold > 0, 1, 0) if m == 0 else 0
        place = 4 * slot + 2 * core + ridge
        return remote(w_ref, got.at[place], sems.at[0], sems.at[1], 2 * (3 * fold + m) + c)

    @pl.when(solver)
    def _():
        for m in range(4):
            for c in range(2):
                mine = (ridge == m) & (core == c)

                @pl.when(jnp.logical_not(mine))
                def _():
                    give(m, c).start()

                @pl.when(mine)
                def _():
                    slot = jnp.where(fold > 0, 1, 0) if m == 0 else 0
                    got[4 * slot + 2 * core + ridge] = w_ref[...]

    def settle(array, count, sem, received):
        c = remote(array.at[pl.ds(0, count)], array.at[pl.ds(0, count)], sems.at[sem], sems.at[sem], me + 1 - 2 * core)
        c.wait_recv() if received else c.wait_send()

    def product(slots):
        for slot in range(slots):
            for b in range(2):
                for r in range(2):
                    value = got[4 * slot + 2 * b + r].astype(F32)
                    rows = pl.ds(64 * slot + 2 * b + r, TRAITS, stride=4)
                    for t in range(4):
                        stacked[4 * b + t, rows, :] = value[:, 128 * t : 128 * t + 128]
        weights = jnp.concatenate([stacked[t, 0 : 64 * slots, :].astype(BF16) for t in range(8)], axis=1)
        return jnp.dot(weights, x_ref[...], preferred_element_type=F32)

    def halves(out, p):
        return jnp.concatenate([out[8 * p : 8 * p + 8, :OUT_LANES], out[8 * p : 8 * p + 8, OUT_LANES:]], axis=0)

    @pl.when(jnp.logical_not(straddles))
    def _():
        @pl.when(solver)
        def _():
            settle(got, 3, 1, True)

        @pl.when(jnp.logical_not(solver))
        def _():
            settle(got, 4, 1, True)

        out = product(1)
        for p in range(8):
            send[p] = halves(out, p).astype(BF16)

    @pl.when(straddles)
    def _():
        settle(got, 7, 1, True)
        out = product(2)
        edge = jnp.int32(0)
        for k in range(1, FOLDS):
            edge = jnp.where(fold == k, bounds()[k], edge)
        half = lax.broadcasted_iota(jnp.int32, (16, OUT_LANES), 0) // 8
        sample = me * ROWS + half * OUT_LANES + lax.broadcasted_iota(jnp.int32, (16, OUT_LANES), 1)
        for p in range(8):
            send[p] = jnp.where(sample >= edge, halves(out, p + 8), halves(out, p)).astype(BF16)

    for d in range(1, 8):
        peer = lax.rem(group + d, 8)
        pltpu.make_async_remote_copy(
            src_ref=send.at[peer], dst_ref=landed.at[group], send_sem=sems.at[2], recv_sem=sems.at[3],
            device_id={"block": peer}, device_id_type=MESH,
        ).start()
    landed[group] = send[group]

    @pl.when(solver)
    def _():
        settle(got, 7, 0, False)

    settle(send, 7, 3, True)
    low = lax.broadcasted_iota(jnp.int32, (8, OUT_LANES), 0) < 4
    for half in range(2):
        value = [landed[p].astype(F32)[8 * half : 8 * half + 8] for p in range(8)]
        for q in range(2):
            tiles = []
            for p in range(0, 8, 2):
                if q == 0:
                    tiles.append(jnp.where(low, value[p], pltpu.roll(value[p + 1], 4, 0)))
                else:
                    tiles.append(jnp.where(low, pltpu.roll(value[p], 4, 0), value[p + 1]))
            out_ref[q, :, OUT_LANES * half : OUT_LANES * (half + 1)] = jnp.concatenate(tiles, axis=0).astype(BF16)
    settle(send, 7, 2, False)


def kernel(
    order_ref, shrink_ref, geno_hbm, pheno_hbm, freq_hbm, out_ref, geno_ref, pheno_ref, freq_ref, in_sem,
    gram_ref, rhs_ref, x_ref, reduce_scratch, solve_scratch, w_ref, predict_scratch,
):
    snps = geno_hbm.shape[0]
    chunks = [slice(at, min(at + 128, snps)) for at in range(0, snps, 128)]
    copies = [pltpu.make_async_copy(geno_hbm.at[c, :], geno_ref.at[c, :], in_sem.at[i]) for i, c in enumerate(chunks)]
    copies += [
        pltpu.make_async_copy(freq_hbm, freq_ref, in_sem.at[8]),
        pltpu.make_async_copy(pheno_hbm, pheno_ref, in_sem.at[9]),
    ]
    for c in copies:
        c.start()
    loaded = [0]

    def load(end):
        while loaded[0] * 128 < end:
            copies[loaded[0]].wait()
            loaded[0] += 1

    me = lax.axis_index("sample")
    group = lax.axis_index("block")
    core = lax.rem(me, 2)
    chip = me // 2
    solver = (lax.rem(chip, 3) < 2) & (chip < 15)
    barrier = pltpu.get_barrier_semaphore()

    def greet(peer):
        pl.semaphore_signal(barrier, inc=1, device_id=peer, device_id_type=MESH)

    greet({"sample": me + 1 - 2 * core})
    for hop in HOPS:
        greet({"sample": 2 * hop_from(chip, hop) + core})
    for d in (-3, -2, -1, 1, 2, 3):
        @pl.when((chip + d >= 0) & (chip + d < CHIPS))
        def _():
            greet({"sample": 2 * (chip + d) + 1 - core})
    for d in range(1, 8):
        greet({"block": lax.rem(group + d, 8)})
    near = lax.min(chip, 3) + lax.min(CHIPS - 1 - chip, 3)

    def barrier_wait():
        pl.semaphore_wait(barrier, CHIPS + 7 + near)

    def settle_inputs():
        copies[8].wait()
        copies[9].wait()

    predict_scratch[1][...] = jnp.zeros_like(predict_scratch[1])
    reduce_part(load, settle_inputs, barrier_wait, order_ref, geno_ref, pheno_ref, freq_ref, gram_ref, rhs_ref, x_ref, *reduce_scratch)

    @pl.when(solver)
    def _():
        count = jnp.int32(1)
        for k in range(FOLDS):
            count = jnp.where(chip // 3 == k, 2 * ROWS * CHIPS - bounds()[k + 1] + bounds()[k], count)
        lam = jnp.where(lax.rem(chip, 3) == 1, shrink_ref[1], shrink_ref[0])
        freq = [
            jnp.concatenate([freq_ref[0:1, b * SNPS : (b + 1) * SNPS], jnp.full((1, WIDE - SNPS), 0.5, F32)], axis=1)
            for b in range(2)
        ]
        own = jnp.where(core == 0, freq[0], freq[1])
        solve_part(lam, count.astype(F32), own, gram_ref, rhs_ref, w_ref, *solve_scratch)

    predict_part(w_ref, x_ref, out_ref, *predict_scratch)


def call(order, shrinkage, geno, pheno, freq):
    dma = pltpu.SemaphoreType.DMA
    rows = CHIPS * SLICE
    return pl.pallas_call(
        kernel,
        out_shape=pltpu.VMEM((2, 32, ROWS), BF16),
        in_specs=[SMEM, SMEM, HBM, HBM, HBM],
        out_specs=VMEM,
        scratch_shapes=[
            pltpu.VMEM((2 * SNPS, ROWS), jnp.int32),
            pltpu.VMEM((TRAITS, ROWS), BF16),
            pltpu.VMEM((1, 2 * SNPS), F32),
            dma((10,)),
            pltpu.VMEM((CHIPS, SLICE, 128), I16),
            pltpu.VMEM((4, TRAITS, 128), F32),
            pltpu.VMEM((2 * WIDE, ROWS), BF16),
            [
                pltpu.VMEM((2, WIDE, ROWS), BF16),
                pltpu.VMEM((TRAITS, ROWS), BF16),
                pltpu.VMEM((2, 2, rows, 128), I16),
                pltpu.VMEM((2, 2, 4, TRAITS, 128), F32),
                pltpu.VMEM((2, rows, 128), I16),
                pltpu.VMEM((2, 4, TRAITS, 128), F32),
                pltpu.VMEM((2 * CHIPS, SLICE, 128), I16),
                pltpu.VMEM((8, TRAITS, 128), F32),
                pltpu.VMEM((2 * CHIPS, SLICE, 128), I16),
                pltpu.VMEM((2 * CHIPS, TRAITS, 128), F32),
                pltpu.VMEM((FOLDS, SLICE, 128), I16),
                pltpu.VMEM((FOLDS, TRAITS, 128), F32),
                dma((4, 2)),
                dma((8,)),
            ],
            [
                pltpu.VMEM((4, W, WIDE), F32),
                pltpu.VMEM((TRAITS, WIDE), F32),
                pltpu.VMEM((4, W, WIDE), F32),
                pltpu.VMEM((W, W), F32),
            ],
            pltpu.VMEM((TRAITS, WIDE), BF16),
            [
                pltpu.VMEM((8, TRAITS, WIDE), BF16),
                pltpu.VMEM((8, 8 * TRAITS, 128), F32),
                pltpu.VMEM((8, 16, OUT_LANES), BF16),
                pltpu.VMEM((8, 16, OUT_LANES), BF16),
                dma((4,)),
            ],
        ],
        compiler_params=pltpu.CompilerParams(collective_id=0, has_side_effects=True, vmem_limit_bytes=LIMIT),
    )(order, shrinkage, geno, pheno, freq)


def shards(genotype, allele_freq, phenotype, shrinkage, owner_order):
    return call(owner_order, shrinkage, genotype.T, phenotype.T, allele_freq.reshape(1, 2 * SNPS))


def solution(mesh):
    in_specs = (P("sample", "block"), P("block"), P("sample", None), P(), P())
    out_specs = P("block", None, "sample")
    return jax.shard_map(shards, mesh=mesh, in_specs=in_specs, out_specs=out_specs, check_vma=False)
```
